128 devices in a mesh: section: 32 (over x, y_hi, z), tp: 4 (over y_lo, core).
Axes of the slice: x: 4, y: 4 (y_hi: 2, y_lo: 2; y = y_hi * 2 + y_lo), z: 4, core: 2. Of those that a mesh axis runs over, the one named last changes fastest.
Arguments:
- arrivals: bfloat16 [32, 256, 4096], P('section'), may hold values from -6 to 6
- grads_in: bfloat16 [32, 256, 4096], P('section'), may hold values from -6 to 6
- stash: bfloat16 [32, 256, 4096], P('section', 'tp'), may hold values from -6 to 6
- gain: float32 [32, 4096], P('section'), may hold values from 0.1 to 1.9
- w_query: bfloat16 [32, 4096, 4096], P('section', None, 'tp'), as said below
- w_key: bfloat16 [32, 4096, 512], P('section', None, 'tp'), as said below
- w_value: bfloat16 [32, 4096, 512], P('section', None, 'tp'), may hold values from -0.09375 to 0.09375
- w_out: bfloat16 [32, 4096, 4096], P('section', 'tp'), may hold values from -0.09375 to 0.09375
Outputs:
- forward_pass: bfloat16 [32, 256, 4096], P('section')
- backward_pass: bfloat16 [32, 256, 4096], P('section')
- evicted: bfloat16 [32, 256, 4096], P('section', 'tp')
- gain_grad: float32 [32, 4096], P('section')
The draws below stay inside these ranges and needn't reach their ends.
Inputs may be any that keep to these rules, and one draw needn't show every extreme that they name: `w_query`: each entry has an independent normal part of standard deviation 4096^-0.5; the 8 query heads of a group may in addition share a column block with their group's key head, of a strength of up to 24 times that; every entry's magnitude stays under 200 * 4096^-0.5. `w_key`: each entry has an independent normal part of standard deviation 4096^-0.5, possibly plus a column block shared with the query heads of its group, of the same standard deviation; every entry's magnitude stays under 16 * 4096^-0.5.
All inputs are finite; a program needn't handle non-finite values.
Results may differ from the reference program's by a relative error of at most 0.0087.
Values may be sent and summed in bfloat16 or wider, within the bound.
A program may use at most 128 MiB of HBM per device.

```python
import math
import jax
import jax.numpy as jnp
from jax import lax

D = 4096
HQ = 32
KV = 4
HD = 128
TOK = 256
SECTIONS = 32


def draw_w_query(key, part):
    key = jax.random.fold_in(key, 21)
    own_key = jax.random.fold_in(key, 0)
    result = jax.random.normal(own_key, (SECTIONS, D, HQ * HD), jnp.float32) * D ** (-0.5)
    return result.astype(jnp.bfloat16)


def draw_w_key(key, part):
    key = jax.random.fold_in(key, 22)
    result = jax.random.normal(key, (SECTIONS, D, KV * HD), jnp.float32) * D ** (-0.5)
    return result.astype(jnp.bfloat16)


def levels(rng, shape, cuts, least, top_value):
    def one(axis_at, blocks):
        heights = jax.random.uniform(jax.random.fold_in(jax.random.fold_in(rng, 6), axis_at), (blocks,), jnp.float32, least / len(cuts), top_value / len(cuts))
        return jnp.repeat(jnp.exp(heights), shape[axis_at] // blocks).reshape((-1,) + (1,) * (len(shape) - axis_at - 1))

    level = one(*cuts[0])
    for cut in cuts[1:]:
        level = level * one(*cut)
    return level


def normal_values(key, shape, deviation, limit, shards=(), dtype=jnp.bfloat16):
    array = deviation * jax.random.normal(key, shape, jnp.float32)
    if shards:
        array = array * levels(key, shape, shards, -0.22, 0.18)
    return jnp.clip(array, -limit, limit).astype(dtype)


def setup_inputs(seed: int = 0) -> dict:
    seeds = jax.random.split(jax.random.key(seed), 9)
    arrivals = normal_values(seeds[0], (SECTIONS, TOK, D), 1.0, 6.0, ((0, 32),))
    grads_in = normal_values(seeds[1], (SECTIONS, TOK, D), 1.0, 6.0, ((0, 32),))
    stash = normal_values(seeds[2], (SECTIONS, TOK, D), 1.0, 6.0, ((0, 32), (1, 4)))
    gain = jnp.clip(1.0 + 0.18 * jax.random.normal(seeds[3], (SECTIONS, D), jnp.float32), 0.1, 1.9)
    w_query = draw_w_query(jax.random.fold_in(seeds[8], 71), 0)
    w_key = draw_w_key(jax.random.fold_in(seeds[8], 71), 0)
    w_value = normal_values(seeds[6], (SECTIONS, D, KV * HD), D ** -0.5, 0.09375, ((0, 32), (2, 4)))
    w_out = normal_values(seeds[7], (SECTIONS, HQ * HD, D), (HQ * HD) ** -0.5, 0.09375, ((0, 32), (1, 4)))
    return {"arrivals": arrivals, "grads_in": grads_in, "stash": stash, "gain": gain, "w_query": w_query, "w_key": w_key, "w_value": w_value, "w_out": w_out}


epsilon = 1e-05

def rotate(heads, sign):
    length = heads.shape[0]
    half = heads.shape[2] // 2
    positions = jnp.arange(length).astype(jnp.float32)
    frequency = jnp.exp(jnp.arange(half).astype(jnp.float32) * (-2.0 * math.log(10000.0) / heads.shape[2]))
    angle = positions[:, None] * frequency[None, :]
    cosine = jnp.cos(angle)[:, None, :]
    sine = sign * jnp.sin(angle)[:, None, :]
    first = heads[..., :half]
    second = heads[..., half:]
    return jnp.concatenate([first * cosine - second * sine, second * cosine + first * sine], axis=-1)

def normalize(inputs, gain):
    values = inputs.astype(jnp.float32)
    inverse_rms = lax.rsqrt(lax.optimization_barrier(jnp.mean(values * values, axis=-1, keepdims=True)) + epsilon)
    scaled = values * inverse_rms
    return (scaled, inverse_rms, (scaled * gain).astype(jnp.bfloat16))

def project(normed, w_query, w_key, w_value):
    length = normed.shape[0]
    query_heads = jnp.dot(normed, w_query, preferred_element_type=jnp.float32).reshape(length, -1, HD)
    key_heads = jnp.dot(normed, w_key, preferred_element_type=jnp.float32).reshape(length, -1, HD)
    value_heads = jnp.dot(normed, w_value, preferred_element_type=jnp.float32).reshape(length, -1, HD)
    return (rotate(query_heads, 1.0).astype(jnp.bfloat16), rotate(key_heads, 1.0).astype(jnp.bfloat16), value_heads.astype(jnp.bfloat16))

def attend(query_heads, key_heads):
    length = query_heads.shape[0]
    groups = key_heads.shape[1]
    grouped = query_heads.reshape(length, groups, -1, HD)
    scores = jnp.einsum('qkge,ske->kgqs', grouped.astype(jnp.float32), key_heads.astype(jnp.float32)) * HD ** (-0.5)
    causal = jnp.arange(length)[:, None] >= jnp.arange(length)[None, :]
    scores = jnp.where(causal, scores, -jnp.inf)
    highest = lax.optimization_barrier(jnp.max(scores, axis=-1, keepdims=True))
    weights = jnp.exp(scores - highest)
    return weights / lax.optimization_barrier(jnp.sum(weights, axis=-1, keepdims=True))

def forward(inputs, gain, w_query, w_key, w_value, w_out):
    scaled, inverse_rms, normed = normalize(inputs, gain)
    query_heads, key_heads, value_heads = project(normed, w_query, w_key, w_value)
    attention = attend(query_heads, key_heads).astype(jnp.bfloat16)
    length = inputs.shape[0]
    context = jnp.einsum('kgqs,ske->qkge', attention.astype(jnp.float32), value_heads.astype(jnp.float32))
    context = context.reshape(length, -1).astype(jnp.bfloat16)
    summed = jnp.dot(context, w_out, preferred_element_type=jnp.float32)
    return (inputs.astype(jnp.float32) + summed).astype(jnp.bfloat16)

def backward(stored, gradient, gain, w_query, w_key, w_value, w_out):
    scaled, inverse_rms, normed = normalize(stored, gain)
    query_heads, key_heads, value_heads = project(normed, w_query, w_key, w_value)
    attention = attend(query_heads, key_heads)
    attention_b = attention.astype(jnp.bfloat16)
    length = stored.shape[0]
    groups = key_heads.shape[1]
    grouped = query_heads.reshape(length, groups, -1, HD)
    d_context = jnp.dot(gradient, w_out.T, preferred_element_type=jnp.float32).astype(jnp.bfloat16)
    d_context = d_context.reshape(length, groups, -1, HD)
    d_probs = jnp.einsum('qkge,ske->kgqs', d_context.astype(jnp.float32), value_heads.astype(jnp.float32))
    d_scores = attention * (d_probs - lax.optimization_barrier(jnp.sum(attention * d_probs, axis=-1, keepdims=True))) * HD ** (-0.5)
    d_scores = d_scores.astype(jnp.bfloat16).astype(jnp.float32)
    d_query = jnp.einsum('kgqs,ske->qkge', d_scores, key_heads.astype(jnp.float32)).reshape(length, -1, HD)
    d_key = jnp.einsum('kgqs,qkge->ske', d_scores, grouped.astype(jnp.float32))
    d_value = jnp.einsum('kgqs,qkge->ske', attention_b.astype(jnp.float32), d_context.astype(jnp.float32))
    d_query = rotate(d_query, -1.0).astype(jnp.bfloat16).reshape(length, -1)
    d_key = rotate(d_key, -1.0).astype(jnp.bfloat16).reshape(length, -1)
    d_value = d_value.astype(jnp.bfloat16).reshape(length, -1)
    d_normed = jnp.dot(d_query, w_query.T, preferred_element_type=jnp.float32)
    d_normed = d_normed + jnp.dot(d_key, w_key.T, preferred_element_type=jnp.float32)
    d_normed = d_normed + jnp.dot(d_value, w_value.T, preferred_element_type=jnp.float32)
    d_gain = lax.optimization_barrier(jnp.sum(d_normed * scaled, axis=0))
    d_unit = d_normed * gain
    d_inputs = gradient.astype(jnp.float32) + inverse_rms * (d_unit - scaled * lax.optimization_barrier(jnp.mean(d_unit * scaled, axis=-1, keepdims=True)))
    return (d_inputs.astype(jnp.bfloat16), d_gain)

def reference(arrivals, grads_in, stash, gain, w_query, w_key, w_value, w_out):

    def one_section(section_items):
        inputs, gradient, stored, section_gain, query_w, key_w, value_w, out_w = section_items
        result = forward(inputs, section_gain, query_w, key_w, value_w, out_w)
        d_inputs, d_gain = backward(stored, gradient, section_gain, query_w, key_w, value_w, out_w)
        return (result, d_inputs, d_gain)
    outputs, gradients, gains = lax.map(one_section, (arrivals, grads_in, stash[::-1], gain, w_query, w_key, w_value, w_out))
    zeros = jnp.zeros_like(outputs[:1])
    forward_pass = jnp.concatenate([zeros, outputs[:-1]], axis=0)
    backward_pass = jnp.concatenate([gradients[1:], zeros], axis=0)
    return (forward_pass, backward_pass, arrivals[::-1], gains)
```

```python
import functools

import jax
import jax.numpy as jnp
import numpy as np
from jax import lax
from jax.experimental import pallas as pl
from jax.experimental.pallas import tpu as pltpu
from jax.sharding import PartitionSpec as P

HD = 128
NC = 8
EPSILON = 1e-05
MESH = pl.DeviceIdType.MESH
NN = (((1,), (0,)), ((), ()))
NT = (((1,), (1,)), ((), ()))
TN = (((0,), (0,)), ((), ()))

ST_M, ST_C, ST_L, ST_F = 0, 1, 2, 3
RS_C, RS_L, HOP, AG_C, AG_L, AG_F = 4, 5, 6, 7, 8, 9
PASS = 6
KINDS = 16


def dot(left, right, dims=NN):
    return lax.dot_general(left, right, dims, preferred_element_type=jnp.float32)


def rope_tables(length):
    half = HD // 2
    frequency = np.exp(np.arange(half, dtype=np.float32) * np.float32(-2.0 * np.log(10000.0) / HD))
    angle = np.arange(length, dtype=np.float32)[:, None] * frequency.astype(np.float32)[None, :]
    cosine, sine = np.cos(angle), np.sin(angle)
    return np.stack(
        [np.concatenate([cosine, cosine], 1), np.concatenate([-sine, sine], 1)]
    ).astype(np.float32)


def kernel(
    sections, tokens, width, heads,
    arr, grd, sth, gain, wq, wk, wv, wo, rope,
    out_f, out_b, evict, out_g,
    w, wob, zf, g, zb, nrm, qkv, ctx, dctx, dqkv, mine, dk, dv, gn, rp, scl, inv, dn, dot_sum,
    sc, rc, sl, rl, hop, gp, gr,
    loc_sem, send_sem, recv_sem, ev_sem, gp_sem,
):
    nq = heads * HD
    rows = tokens // 4
    cw = width // NC
    s = lax.axis_index("section")
    t = lax.axis_index("tp")
    t_core = t + 1 - 2 * (t % 2)
    t_lo = (t + 2) % 4
    t_diag = (t_core + 2) % 4
    last_z = (s % 4) // 3
    first_z = ((s + 3) % 4) // 3
    t_next = (t + 2 * last_z) % 4
    t_prev = (t + 2 * first_z) % 4
    p_core = (s, t_core)
    p_lo = (s, t_lo)
    p_mir = (sections - 1 - s, t_lo)
    p_next = ((s + 1) % sections, t_next)
    p_prev = ((s + sections - 1) % sections, t_prev)

    def block(index):
        return pl.ds(pl.multiple_of(index * rows, rows), rows)

    def chunk(n):
        return pl.ds(pl.multiple_of(n * cw, cw), cw)

    def remote(src, dst, kind, n, device):
        return pltpu.make_async_remote_copy(
            src_ref=src, dst_ref=dst, send_sem=send_sem.at[kind, n], recv_sem=recv_sem.at[kind, n],
            device_id=device, device_id_type=MESH,
        )

    tile = 256
    tiles = nq // tile

    def load(src, dst, n):
        return pltpu.make_async_copy(src, dst, loc_sem.at[n])

    loads = [
        load(arr.at[0], zf, 0),
        load(gain, gn, 1),
        load(wk.at[0], w.at[:, pl.ds(nq, HD)], 2),
        load(wv.at[0], w.at[:, pl.ds(nq + HD, HD)], 3),
        load(rope, rp, 4),
        load(grd.at[0], g, 5),
        load(wo.at[0], wob, 6),
    ]

    def load_q(n):
        cols = pl.ds(pl.multiple_of(n * tile, tile), tile)
        return load(wq.at[0, :, cols], w.at[:, cols], 7 + n)

    loads[0].start()
    loads[1].start()
    loads[4].start()
    for n in range(tiles):
        load_q(n).start()
    loads[2].start()
    loads[3].start()
    loads[5].start()
    loads[6].start()

    barrier = pltpu.get_barrier_semaphore()
    for device in (p_core, p_lo, p_mir, p_next, p_prev):
        pl.semaphore_signal(barrier, inc=1, device_id=device, device_id_type=MESH)
    pl.semaphore_wait(barrier, 5)

    def st_m(n, at):
        return remote(sth.at[0, :, chunk(n)], zb.at[block(at), chunk(n)], ST_M, n, p_mir)

    def st_c(n, at):
        return remote(zb.at[block(t_lo), chunk(n)], zb.at[block(at), chunk(n)], ST_C, n, p_core)

    def st_l(n, at):
        return remote(zb.at[block(t_lo), chunk(n)], zb.at[block(at), chunk(n)], ST_L, n, p_lo)

    def st_f(n, at):
        return remote(zb.at[block(t), chunk(n)], zb.at[block(at), chunk(n)], ST_F, n, p_core)

    def each(count, body):
        lax.fori_loop(0, count, lambda i, c: (body(i), c)[1], 0)

    each(NC, lambda n: st_m(n, t).start())

    def stash_spread(n):
        st_m(n, t_lo).wait_recv()
        st_l(n, t_lo).start()
        st_c(n, t_lo).start()

    def stash_forward(n):
        st_l(n, t).wait_recv()
        st_f(n, t).start()

    def stash_last(n):
        st_c(n, t_diag).wait_recv()
        st_f(n, t_core).wait_recv()

    evicted = pltpu.make_async_remote_copy(
        src_ref=arr.at[0, block(t_lo)], dst_ref=evict.at[0], send_sem=ev_sem.at[0],
        recv_sem=ev_sem.at[1], device_id=p_mir, device_id_type=MESH,
    )

    step = 16

    def normalize(src):
        def body(i):
            at = pl.ds(pl.multiple_of(i * step, step), step)
            x = src[at].astype(jnp.float32)
            inverse = lax.rsqrt(jnp.mean(x * x, axis=-1, keepdims=True) + EPSILON)
            x = src[at].astype(jnp.float32)
            nrm[at] = (x * inverse * gn[...]).astype(jnp.bfloat16)

        each(tokens // step, body)

    def turn(x, sign):
        return x * rp[0] + pltpu.roll(x, HD // 2, 1) * (sign * rp[1])

    def project_q(n):
        cols = pl.ds(pl.multiple_of(n * tile, tile), tile)
        y = dot(nrm[...], w[:, cols])
        y = jnp.concatenate(
            [turn(y[:, i * HD:(i + 1) * HD], 1.0) for i in range(tile // HD)], axis=1
        )
        qkv[:, cols] = y.astype(jnp.bfloat16)

    def project_kv():
        y = dot(nrm[...], w[:, nq:])
        qkv[:, nq:nq + HD] = turn(y[:, :HD], 1.0).astype(jnp.bfloat16)
        qkv[:, nq + HD:] = y[:, HD:].astype(jnp.bfloat16)

    def place(b):
        low = (b % 2 + t % 2) % 2
        high = (b // 2 + t // 2) % 2
        return block(2 * low + high)

    def put(ref, cols, value):
        for b in range(4):
            ref[place(b), cols] = value[b * rows:(b + 1) * rows]

    def head_cols(h):
        return pl.ds(pl.multiple_of(h * HD, HD), HD)

    scale = HD ** (-0.5)

    def attend(h):
        cols = head_cols(h)
        scores = dot(qkv[:, cols], qkv[:, nq:nq + HD], NT) * scale
        q_at = lax.broadcasted_iota(jnp.int32, scores.shape, 0)
        k_at = lax.broadcasted_iota(jnp.int32, scores.shape, 1)
        scores = jnp.where(q_at >= k_at, scores, -jnp.inf)
        e = jnp.exp(scores - jnp.max(scores, axis=1, keepdims=True))
        probs = e / jnp.sum(e, axis=1, keepdims=True)
        out = dot(probs.astype(jnp.bfloat16), qkv[:, nq + HD:])
        put(ctx, cols, out.astype(jnp.bfloat16))

    def attend_back(h):
        cols = head_cols(h)
        q, k, v = qkv[:, cols], qkv[:, nq:nq + HD], qkv[:, nq + HD:]
        dc = dctx[:, cols]
        scores = dot(k, q, NT) * scale
        k_at = lax.broadcasted_iota(jnp.int32, scores.shape, 0)
        q_at = lax.broadcasted_iota(jnp.int32, scores.shape, 1)
        scores = jnp.where(q_at >= k_at, scores, -jnp.inf)
        e = jnp.exp(scores - jnp.max(scores, axis=0, keepdims=True))
        probs = e / jnp.sum(e, axis=0, keepdims=True)
        d_probs = dot(v, dc, NT)
        inner = jnp.sum(probs * d_probs, axis=0, keepdims=True)
        d_scores = (probs * (d_probs - inner) * scale).astype(jnp.bfloat16)
        dk[...] += dot(d_scores, q)
        dv[...] += dot(probs.astype(jnp.bfloat16), dc)
        put(dqkv, cols, turn(dot(d_scores, k, TN), -1.0).astype(jnp.bfloat16))

    def context_back(n):
        cols = pl.ds(pl.multiple_of(n * tile, tile), tile)
        dctx[:, cols] = dot(g[...], wob[cols, :], NT).astype(jnp.bfloat16)

    def rs_core(f, n):
        return remote(sc.at[f, n], rc.at[f, n], RS_C + PASS * f, n, p_core)

    def rs_lo(f, n):
        return remote(sl.at[f, n], rl.at[f, n], RS_L + PASS * f, n, p_lo)

    def sum_send(f, n, part):
        sc[f, n] = part[2 * rows:].astype(jnp.bfloat16)
        rs_core(f, n).start()
        mine[:, chunk(n)] = part[:2 * rows]

    def sum_core(f, n):
        rs_core(f, n).wait_recv()
        total = mine[:, chunk(n)] + rc[f, n].astype(jnp.float32)
        sl[f, n] = total[rows:].astype(jnp.bfloat16)
        rs_lo(f, n).start()
        mine[:rows, chunk(n)] = total[:rows]

    def sum_lo(f, n):
        rs_lo(f, n).wait_recv()
        return mine[:rows, chunk(n)] + rl[f, n].astype(jnp.float32)

    outs = (out_f, out_b)
    hops = (p_next, p_prev)
    came = ((t + 2 * first_z) % 4, (t + 2 * last_z) % 4)

    def at_out(f, b, n):
        return outs[f].at[0, block(b), chunk(n)]

    def hop_copy(f, n, b):
        return remote(hop.at[f, :, chunk(n)], at_out(f, b, n), HOP + PASS * f, n, hops[f])

    def ag(f, n, kind, b, to):
        return remote(at_out(f, b, n), at_out(f, b, n), kind + PASS * f, n, to)

    def flip_core(b):
        return b + 1 - 2 * (b % 2)

    def flip_lo(b):
        return (b + 2) % 4

    def spread(f, n):
        b = came[f]
        hop_copy(f, n, b).wait_recv()
        ag(f, n, AG_L, b, p_lo).start()
        ag(f, n, AG_C, b, p_core).start()

    def forward(f, n):
        b = flip_lo(came[f])
        ag(f, n, AG_L, b, p_lo).wait_recv()
        ag(f, n, AG_F, b, p_core).start()

    def collect(f, n):
        b = flip_core(came[f])
        ag(f, n, AG_C, b, p_core).wait_recv()
        ag(f, n, AG_F, flip_lo(b), p_core).wait_recv()

    def finish_f(n):
        y = zf[block(t), chunk(n)].astype(jnp.float32) + sum_lo(0, n)
        y = jnp.where(s == sections - 1, jnp.zeros_like(y), y)
        hop[0, :, chunk(n)] = y.astype(jnp.bfloat16)
        hop_copy(0, n, t).start()

    loads[0].wait()
    loads[1].wait()
    normalize(zf)
    loads[4].wait()

    def run_project(i):
        load_q(i).wait()
        project_q(i)
        stash_spread(i)

    each(tiles, run_project)
    loads[2].wait()
    loads[3].wait()
    project_kv()
    loads[5].wait()
    loads[6].wait()

    def run_context_back(i):
        context_back(i)
        stash_spread(NC - tiles + i)

    each(tiles, run_context_back)
    evicted.start()

    def run_attend(h):
        attend(h)
        stash_forward(h)

    each(heads, run_attend)

    def run_out(n):
        sum_send(0, n, dot(ctx[...], wob[:, chunk(n)]))

        @pl.when(n > 0)
        def _():
            sum_core(0, n - 1)

    each(NC, run_out)
    sum_core(0, NC - 1)

    each(NC, stash_last)
    normalize(zb)

    def run_project_b(i):
        project_q(i)
        finish_f(i)

    each(tiles, run_project_b)
    project_kv()
    dk[...] = jnp.zeros_like(dk)
    dv[...] = jnp.zeros_like(dv)

    def run_attend_back(h):
        attend_back(h)

        @pl.when(h < NC - tiles)
        def _():
            finish_f(tiles + h)

        spread(0, h)

    each(heads, run_attend_back)
    put(dqkv, pl.ds(nq, HD), turn(dk[...], -1.0).astype(jnp.bfloat16))
    put(dqkv, pl.ds(nq + HD, HD), dv[...].astype(jnp.bfloat16))

    def run_d_normed(n):
        sum_send(1, n, dot(dqkv[...], w[chunk(n), :], NT))

        @pl.when(n > 0)
        def _():
            sum_core(1, n - 1)

        forward(0, n)

    each(NC, run_d_normed)
    sum_core(1, NC - 1)

    def own_scaled(i):
        at = pl.ds(pl.multiple_of(t * rows + i * step, step), step)
        to = pl.ds(pl.multiple_of(i * step, step), step)
        x = zb[at].astype(jnp.float32)
        inverse = lax.rsqrt(jnp.mean(x * x, axis=-1, keepdims=True) + EPSILON)
        x = zb[at].astype(jnp.float32)
        scl[to] = x * inverse
        inv[to] = jnp.broadcast_to(inverse, (step, HD))

    each(rows // step, own_scaled)
    dot_sum[...] = jnp.zeros_like(dot_sum)

    def run_norm_back(n):
        d = sum_lo(1, n)
        product = d * scl[:, chunk(n)]
        gp[0, :, chunk(n)] = jnp.sum(product, axis=0, keepdims=True)
        unit = d * gn[:, chunk(n)]
        dn[:, chunk(n)] = unit
        dot_sum[...] += jnp.broadcast_to(
            jnp.sum(unit * scl[:, chunk(n)], axis=1, keepdims=True), dot_sum.shape
        )

    each(NC, run_norm_back)

    def gain_copy(i, to):
        return pltpu.make_async_remote_copy(
            src_ref=gp.at[i], dst_ref=gr.at[i], send_sem=gp_sem.at[2 * i],
            recv_sem=gp_sem.at[2 * i + 1], device_id=to, device_id_type=MESH,
        )

    gain_copy(0, p_core).start()

    def send_back(n):
        mean = dot_sum[:, :1] * (1.0 / width)
        dz = g[block(t), chunk(n)].astype(jnp.float32) + inv[:, :1] * (
            dn[:, chunk(n)] - scl[:, chunk(n)] * mean
        )
        dz = jnp.where(s == 0, jnp.zeros_like(dz), dz)
        hop[1, :, chunk(n)] = dz.astype(jnp.bfloat16)
        hop_copy(1, n, t).start()

    each(NC, send_back)
    gain_copy(0, p_core).wait_recv()
    gp[1] = gp[0] + gr[0]
    gain_copy(1, p_lo).start()

    def run_tail(n):
        spread(1, n)

        @pl.when(n > 1)
        def _():
            forward(1, n - 2)

    each(NC, run_tail)
    forward(1, NC - 2)
    forward(1, NC - 1)
    gain_copy(1, p_lo).wait_recv()
    gp[2] = gp[1] + gr[1]
    gain_out = pltpu.make_async_copy(gp.at[2], out_g, loc_sem.at[0])
    gain_out.start()

    def drain(n):
        collect(0, n)
        collect(1, n)
        st_m(n, t).wait_send()
        st_c(n, t_lo).wait_send()
        st_l(n, t_lo).wait_send()
        st_f(n, t).wait_send()
        for f in range(2):
            rs_core(f, n).wait_send()
            rs_lo(f, n).wait_send()
            hop_copy(f, n, t).wait_send()
            ag(f, n, AG_L, came[f], p_lo).wait_send()
            ag(f, n, AG_C, came[f], p_core).wait_send()
            ag(f, n, AG_F, flip_lo(came[f]), p_core).wait_send()

    each(NC, drain)
    evicted.wait()
    gain_copy(0, p_core).wait_send()
    gain_copy(1, p_lo).wait_send()
    gain_out.wait()


def shards(sections, arrivals, grads_in, stash, gain, w_query, w_key, w_value, w_out):
    _, tokens, width = arrivals.shape
    nq = w_query.shape[2]
    heads = nq // HD
    rows = tokens // 4
    nw = nq + 2 * HD
    cw = width // NC
    f32, bf16 = jnp.float32, jnp.bfloat16
    scratch = [
        pltpu.VMEM((width, nw), bf16),
        pltpu.VMEM((nq, width), bf16),
        pltpu.VMEM((tokens, width), bf16),
        pltpu.VMEM((tokens, width), bf16),
        pltpu.VMEM((tokens, width), bf16),
        pltpu.VMEM((tokens, width), bf16),
        pltpu.VMEM((tokens, nw), bf16),
        pltpu.VMEM((tokens, nq), bf16),
        pltpu.VMEM((tokens, nq), bf16),
        pltpu.VMEM((tokens, nw), bf16),
        pltpu.VMEM((2 * rows, width), f32),
        pltpu.VMEM((tokens, HD), f32),
        pltpu.VMEM((tokens, HD), f32),
        pltpu.VMEM((1, width), f32),
        pltpu.VMEM((2, tokens, HD), f32),
        pltpu.VMEM((rows, width), f32),
        pltpu.VMEM((rows, HD), f32),
        pltpu.VMEM((rows, width), f32),
        pltpu.VMEM((rows, HD), f32),
        pltpu.VMEM((2, NC, 2 * rows, cw), bf16),
        pltpu.VMEM((2, NC, 2 * rows, cw), bf16),
        pltpu.VMEM((2, NC, rows, cw), bf16),
        pltpu.VMEM((2, NC, rows, cw), bf16),
        pltpu.VMEM((2, rows, width), bf16),
        pltpu.VMEM((3, 1, width), f32),
        pltpu.VMEM((2, 1, width), f32),
        pltpu.SemaphoreType.DMA((7 + nq // 256,)),
        pltpu.SemaphoreType.DMA((KINDS, NC)),
        pltpu.SemaphoreType.DMA((KINDS, NC)),
        pltpu.SemaphoreType.DMA((2,)),
        pltpu.SemaphoreType.DMA((4,)),
    ]
    any_spec = pl.BlockSpec(memory_space=pl.ANY)
    flops = 2 * tokens * width * (2 * nw + 2 * nq + nw)
    outs = pl.pallas_call(
        functools.partial(kernel, sections, tokens, width, heads),
        out_shape=(
            jax.ShapeDtypeStruct((1, tokens, width), bf16),
            jax.ShapeDtypeStruct((1, tokens, width), bf16),
            jax.ShapeDtypeStruct((1, rows, width), bf16),
            jax.ShapeDtypeStruct((1, width), f32),
        ),
        in_specs=[any_spec] * 9,
        out_specs=(any_spec,) * 4,
        scratch_shapes=scratch,
        compiler_params=pltpu.CompilerParams(
            collective_id=0, has_side_effects=True, vmem_limit_bytes=60 * 1024 * 1024
        ),
        cost_estimate=pl.CostEstimate(
            flops=flops, bytes_accessed=2 * width * (2 * nw + 6 * tokens), transcendentals=0
        ),
    )(arrivals, grads_in, stash, gain, w_query, w_key, w_value, w_out, jnp.asarray(rope_tables(tokens)))
    return outs


def solution(mesh):
    in_specs = (
        P("section", None, None),
        P("section", None, None),
        P("section", "tp", None),
        P("section", None),
        P("section", None, "tp"),
        P("section", None, "tp"),
        P("section", None, "tp"),
        P("section", "tp", None),
    )
    out_specs = (
        P("section", None, None),
        P("section", None, None),
        P("section", "tp", None),
        P("section", None),
    )
    body = functools.partial(shards, mesh.shape["section"])
    return jax.shard_map(body, mesh=mesh, in_specs=in_specs, out_specs=out_specs, check_vma=False)
```

```python
import functools

import jax
import jax.numpy as jnp
import numpy as np
from jax import lax
from jax.experimental import pallas as pl
from jax.experimental.pallas import tpu as pltpu
from jax.sharding import PartitionSpec as P

HD = 128
LOG2E = 1.4426950408889634
NC = 8
PAIR = 2
NH = NC // 2
EPSILON = 1e-05
MESH = pl.DeviceIdType.MESH
NN = (((1,), (0,)), ((), ()))
NT = (((1,), (1,)), ((), ()))
TN = (((0,), (0,)), ((), ()))

ST_M, ST_C, ST_L, ST_F = 0, 1, 2, 3
RS_C, RS_L, HOP, AG_C, AG_L, AG_F = 4, 5, 6, 7, 8, 9
PASS = 6
KINDS = 16


def dot(left, right, dims=NN):
    return lax.dot_general(left, right, dims, preferred_element_type=jnp.float32)


def rope_tables(length):
    half = HD // 2
    frequency = np.exp(np.arange(half, dtype=np.float32) * np.float32(-2.0 * np.log(10000.0) / HD))
    angle = np.arange(length, dtype=np.float32)[:, None] * frequency.astype(np.float32)[None, :]
    cosine, sine = np.cos(angle), np.sin(angle)
    return np.stack(
        [np.concatenate([cosine, cosine], 1), np.concatenate([-sine, sine], 1)]
    ).astype(np.float32)


def kernel(
    sections, tokens, width, heads,
    arr, grd, sth, gain, wq, wk, wv, wo, rope,
    out_f, out_b, evict, out_g,
    w, wob, zf, g, zb, nrm, qkv, ctx, dctx, dqkv, mine, dk, dv, gn, rp, scl, inv, dn, dot_sum,
    sc_f, rc_f, sl_f, rl_f, sc_b, rc_b, sl_b, rl_b, hop, gp, gr,
    loc_sem, send_sem, recv_sem, ev_sem, gp_sem,
):
    nq = heads * HD
    rows = tokens // 4
    cw = width // NC
    s = lax.axis_index("section")
    t = lax.axis_index("tp")
    t_core = t + 1 - 2 * (t % 2)
    t_lo = (t + 2) % 4
    t_diag = (t_core + 2) % 4
    last_z = (s % 4) // 3
    first_z = ((s + 3) % 4) // 3
    t_next = (t + 2 * last_z) % 4
    t_prev = (t + 2 * first_z) % 4
    p_core = (s, t_core)
    p_lo = (s, t_lo)
    p_mir = (sections - 1 - s, t_lo)
    p_next = ((s + 1) % sections, t_next)
    p_prev = ((s + sections - 1) % sections, t_prev)

    def block(index):
        return pl.ds(pl.multiple_of(index * rows, rows), rows)

    def chunk(n):
        return pl.ds(pl.multiple_of(n * cw, cw), cw)

    def remote(src, dst, kind, n, device):
        return pltpu.make_async_remote_copy(
            src_ref=src, dst_ref=dst, send_sem=send_sem.at[kind, n], recv_sem=recv_sem.at[kind, n],
            device_id=device, device_id_type=MESH,
        )

    tile = 256
    tiles = nq // tile

    def load(src, dst, n):
        return pltpu.make_async_copy(src, dst, loc_sem.at[n])

    loads = [
        load(arr.at[0], zf, 0),
        load(gain, gn, 1),
        load(wk.at[0], w.at[:, pl.ds(nq, HD)], 2),
        load(wv.at[0], w.at[:, pl.ds(nq + HD, HD)], 3),
        load(rope, rp, 4),
        load(grd.at[0], g, 5),
        load(wo.at[0], wob, 6),
    ]

    def load_q(n):
        cols = pl.ds(pl.multiple_of(n * tile, tile), tile)
        return load(wq.at[0, :, cols], w.at[:, cols], 7 + n)

    loads[0].start()
    loads[1].start()
    loads[4].start()

    barrier = pltpu.get_barrier_semaphore()
    for device in (p_core, p_lo, p_mir, p_next, p_prev):
        pl.semaphore_signal(barrier, inc=1, device_id=device, device_id_type=MESH)
    pl.semaphore_wait(barrier, 5)

    def st_m(n, at):
        return remote(sth.at[0, :, chunk(n)], zb.at[block(at), chunk(n)], ST_M, n, p_mir)

    def st_c(n, at):
        return remote(zb.at[block(t_lo), chunk(n)], zb.at[block(at), chunk(n)], ST_C, n, p_core)

    def st_l(n, at):
        return remote(zb.at[block(t_lo), chunk(n)], zb.at[block(at), chunk(n)], ST_L, n, p_lo)

    def st_f(n, at):
        return remote(zb.at[block(t), chunk(n)], zb.at[block(at), chunk(n)], ST_F, n, p_core)

    def each(count, body):
        lax.fori_loop(0, count, lambda i, c: (body(i), c)[1], 0)

    each(NC, lambda n: st_m(n, t).start())
    for n in range(tiles):
        load_q(n).start()
    loads[2].start()
    loads[3].start()

    def stash_spread(n):
        st_m(n, t_lo).wait_recv()
        st_l(n, t_lo).start()
        st_c(n, t_lo).start()

    def stash_forward(n):
        st_l(n, t).wait_recv()
        st_f(n, t).start()

    def stash_last(n):
        st_c(n, t_diag).wait_recv()
        st_f(n, t_core).wait_recv()

    evicted = pltpu.make_async_remote_copy(
        src_ref=arr.at[0, block(t_lo)], dst_ref=evict.at[0], send_sem=ev_sem.at[0],
        recv_sem=ev_sem.at[1], device_id=p_mir, device_id_type=MESH,
    )

    evicted.start()

    step = 16

    def normalize(src):
        def body(i):
            at = pl.ds(pl.multiple_of(i * step, step), step)
            x = src[at].astype(jnp.float32)
            inverse = lax.rsqrt(jnp.mean(x * x, axis=-1, keepdims=True) + EPSILON)
            x = src[at].astype(jnp.float32)
            nrm[at] = (x * inverse * gn[...]).astype(jnp.bfloat16)

        each(tokens // step, body)

    def turn(x, sign):
        return x * rp[0] + pltpu.roll(x, HD // 2, 1) * (sign * rp[1])

    def project_q(n):
        cols = pl.ds(pl.multiple_of(n * tile, tile), tile)
        y = dot(nrm[...], w[:, cols])
        y = jnp.concatenate(
            [turn(y[:, i * HD:(i + 1) * HD], 1.0) for i in range(tile // HD)], axis=1
        )
        qkv[:, cols] = y.astype(jnp.bfloat16)

    def project_kv():
        y = dot(nrm[...], w[:, nq:])
        qkv[:, nq:nq + HD] = turn(y[:, :HD], 1.0).astype(jnp.bfloat16)
        qkv[:, nq + HD:] = y[:, HD:].astype(jnp.bfloat16)

    def place(b):
        low = (b % 2 + t % 2) % 2
        high = (b // 2 + t // 2) % 2
        return 2 * low + high

    def put(cols, value):
        for b in range(4):
            ctx[block(place(b)), cols] = value[b * rows:(b + 1) * rows]

    def put_back(cols, value):
        part = rows // 2
        for b in range(4):
            for half in range(2):
                at = place(b)
                at = (at // 2) * 2 * rows + half * rows + (at % 2) * part
                to = pl.ds(pl.multiple_of(at, part), part)
                dqkv[to, cols] = value[b * rows + half * part:b * rows + (half + 1) * part]

    def head_cols(h):
        return pl.ds(pl.multiple_of(h * HD, HD), HD)

    scale = HD ** (-0.5)
    mid = tokens // 2
    bfloat = jnp.bfloat16

    def softmax(scores, axis):
        highest = jnp.max(scores, axis=axis, keepdims=True)
        e = jnp.exp2((scores - highest) * (scale * LOG2E))
        return e * (1.0 / jnp.sum(e, axis=axis, keepdims=True))

    def causal(scores, q_axis):
        q_at = lax.broadcasted_iota(jnp.int32, scores.shape, q_axis)
        k_at = lax.broadcasted_iota(jnp.int32, scores.shape, 1 - q_axis)
        return jnp.where(q_at >= k_at, scores, -jnp.inf)

    def attend(h):
        cols = head_cols(h)
        q, k, v = qkv[:, cols], qkv[:, nq:nq + HD], qkv[:, nq + HD:]
        early = softmax(causal(dot(q[:mid], k[:mid], NT), 0), 1)
        late = dot(q[mid:], k, NT)
        late = softmax(jnp.concatenate([late[:, :mid], causal(late[:, mid:], 0)], axis=1), 1)
        out = jnp.concatenate(
            [dot(early.astype(bfloat), v[:mid]), dot(late.astype(bfloat), v)], axis=0
        )
        put(cols, out.astype(bfloat))

    def attend_back(h):
        cols = head_cols(h)
        q, k, v = qkv[:, cols], qkv[:, nq:nq + HD], qkv[:, nq + HD:]
        dc = dctx[:, cols]

        def half(scores, d_probs):
            probs = softmax(scores, 0)
            inner = jnp.sum(probs * d_probs, axis=0, keepdims=True)
            return probs.astype(bfloat), (probs * (d_probs - inner) * scale).astype(bfloat)

        p_early, s_early = half(causal(dot(k[:mid], q[:mid], NT), 1), dot(v[:mid], dc[:mid], NT))
        late = dot(k, q[mid:], NT)
        late = jnp.concatenate([late[:mid], causal(late[mid:], 1)], axis=0)
        p_late, s_late = half(late, dot(v, dc[mid:], NT))

        def whole(first, second):
            first = jnp.concatenate([first, jnp.zeros_like(first)], axis=0)
            return jnp.concatenate([first, second], axis=1)

        d_scores = whole(s_early, s_late)
        dk[...] += dot(d_scores, q)
        dv[...] += dot(whole(p_early, p_late), dc)
        put_back(cols, turn(dot(d_scores, k, TN), -1.0).astype(bfloat))

    def context_back(n):
        cols = pl.ds(pl.multiple_of(n * tile, tile), tile)
        dctx[:, cols] = dot(g[...], wob[cols, :], NT).astype(jnp.bfloat16)

    sc, rc, sl, rl = (sc_f, sc_b), (rc_f, rc_b), (sl_f, sl_b), (rl_f, rl_b)

    def extent(f, n):
        if f == 0:
            return 0, rows, chunk(n), 0
        half = n // NH
        cols = pl.ds(pl.multiple_of((n % NH) * (width // NH), width // NH), width // NH)
        first = pl.multiple_of(half * (rows // 2), rows // 2)
        return first, rows // 2, cols, pl.multiple_of(half * rows, rows)

    def rs_core(f, n):
        return remote(sc[f].at[n], rc[f].at[n], RS_C + PASS * f, n, p_core)

    def rs_lo(f, n):
        return remote(sl[f].at[n], rl[f].at[n], RS_L + PASS * f, n, p_lo)

    def sum_send(f, n, part):
        sc[f][n] = part[2 * rows:].astype(jnp.bfloat16)
        rs_core(f, n).start()
        mine[:, chunk(n)] = part[:2 * rows]

    def sum_core(n):
        rs_core(0, n).wait_recv()
        total = mine[:, chunk(n)] + rc_f[n].astype(jnp.float32)
        sl_f[n] = total[rows:].astype(jnp.bfloat16)
        rs_lo(0, n).start()
        mine[:rows, chunk(n)] = total[:rows]

    def sum_core_back(n):
        rs_core(1, n).wait_recv()
        total = mine[:, chunk(n)] + rc_b[n].astype(jnp.float32)
        part = rows // 2
        cols = pl.ds(pl.multiple_of((n % 2) * cw, cw), cw)
        for half in range(2):
            at = half * rows
            sl_b[half * NH + n // 2, :, cols] = total[at + part:at + rows].astype(jnp.bfloat16)
            mine[at:at + part, chunk(n)] = total[at:at + part]

    def sum_lo(f, n):
        _, count, cols, at = extent(f, n)
        rs_lo(f, n).wait_recv()
        return mine[pl.ds(at, count), cols] + rl[f][n].astype(jnp.float32)

    outs = (out_f, out_b)
    hops = (p_next, p_prev)
    came = ((t + 2 * first_z) % 4, (t + 2 * last_z) % 4)

    def at_out(f, b, n):
        first, count, cols, _ = extent(f, n)
        return outs[f].at[0, pl.ds(pl.multiple_of(b * rows + first, count), count), cols]

    def hop_copy(f, n, b):
        first, count, cols, _ = extent(f, n)
        src = hop.at[f, pl.ds(first, count), cols]
        return remote(src, at_out(f, b, n), HOP + PASS * f, n, hops[f])

    def ag(f, n, kind, b, to):
        return remote(at_out(f, b, n), at_out(f, b, n), kind + PASS * f, n, to)

    def flip_core(b):
        return b + 1 - 2 * (b % 2)

    def flip_lo(b):
        return (b + 2) % 4

    def spread(f, n):
        b = came[f]
        hop_copy(f, n, b).wait_recv()
        ag(f, n, AG_L, b, p_lo).start()
        ag(f, n, AG_C, b, p_core).start()

    def forward(f, n):
        b = flip_lo(came[f])
        ag(f, n, AG_L, b, p_lo).wait_recv()
        ag(f, n, AG_F, b, p_core).start()

    def collect(f, n):
        b = flip_core(came[f])
        ag(f, n, AG_C, b, p_core).wait_recv()
        ag(f, n, AG_F, flip_lo(b), p_core).wait_recv()

    def spread_f(n):
        spread(0, n)

    def forward_f(n):
        forward(0, n)

    def finish_f(n):
        y = zf[block(t), chunk(n)].astype(jnp.float32) + sum_lo(0, n)
        y = jnp.where(s == sections - 1, jnp.zeros_like(y), y)
        hop[0, :, chunk(n)] = y.astype(jnp.bfloat16)
        hop_copy(0, n, t).start()

    def loop(count, body, after):
        def both(i):
            body(i)
            for at, steps in after.items():

                @pl.when(i == at)
                def _():
                    for act, n in steps:
                        act(n)

        each(count, both)

    def heads_of(body):
        def several(i):
            for k in range(PAIR):
                body(PAIR * i + k)

        return several

    loads[0].wait()
    loads[1].wait()
    normalize(zf)
    loads[6].start()
    loads[5].start()
    loads[4].wait()

    def run_project(i):
        load_q(i).wait()
        project_q(i)

    each(tiles, run_project)
    loads[2].wait()
    loads[3].wait()
    project_kv()
    stash_spread(0)
    loop(heads // PAIR, heads_of(attend), {i: [(stash_spread, i + 1)] for i in range(4)})
    loads[5].wait()
    loads[6].wait()
    loop(tiles, context_back, {1: [(stash_spread, 5)], 3: [(stash_spread, 6)]})

    def run_out(n):
        sum_send(0, n, dot(ctx[...], wob[:, chunk(n)]))

        @pl.when(n > 0)
        def _():
            sum_core(n - 1)

        @pl.when(n == 2)
        def _():
            stash_spread(NC - 1)

        stash_forward(n)

    each(NC, run_out)
    sum_core(NC - 1)
    each(NC, stash_last)
    normalize(zb)
    finish_f(0)
    finish_f(1)
    loop(tiles, project_q, {
        0: [(finish_f, 2)],
        1: [(finish_f, 3)],
        2: [(finish_f, 4), (spread_f, 0)],
        3: [(finish_f, 5), (spread_f, 1)],
    })
    project_kv()
    dk[...] = jnp.zeros_like(dk)
    dv[...] = jnp.zeros_like(dv)
    loop(heads // PAIR, heads_of(attend_back), {
        0: [(finish_f, 6), (finish_f, 7), (spread_f, 2)],
        1: [(spread_f, 3), (spread_f, 4)],
        2: [(spread_f, 5), (spread_f, 6)],
        3: [(spread_f, 7)],
    })
    put_back(pl.ds(nq, HD), turn(dk[...], -1.0).astype(jnp.bfloat16))
    put_back(pl.ds(nq + HD, HD), dv[...].astype(jnp.bfloat16))

    def run_d_normed(n):
        sum_send(1, n, dot(dqkv[...], w[chunk(n), :], NT))

        @pl.when(n > 0)
        def _():
            sum_core_back(n - 1)

            @pl.when(n % 2 == 0)
            def _():
                rs_lo(1, n // 2 - 1).start()

    each(NC, run_d_normed)
    sum_core_back(NC - 1)
    for n in range(NH - 1, NC):
        rs_lo(1, n).start()

    def own_scaled(i):
        at = pl.ds(pl.multiple_of(t * rows + i * step, step), step)
        to = pl.ds(pl.multiple_of(i * step, step), step)
        x = zb[at].astype(jnp.float32)
        inverse = lax.rsqrt(jnp.mean(x * x, axis=-1, keepdims=True) + EPSILON)
        x = zb[at].astype(jnp.float32)
        scl[to] = x * inverse
        inv[to] = jnp.broadcast_to(inverse, (step, HD))

    each(rows // step, own_scaled)
    dot_sum[...] = jnp.zeros_like(dot_sum)
    gp[0] = jnp.zeros((1, width), jnp.float32)
    each(NC, forward_f)

    def run_norm_back(n):
        first, count, cols, _ = extent(1, n)
        at = pl.ds(first, count)
        d = sum_lo(1, n)
        scaled = scl[at, cols]
        gp[0, :, cols] += jnp.sum(d * scaled, axis=0, keepdims=True)
        unit = d * gn[:, cols]
        dn[at, cols] = unit
        dot_sum[at] += jnp.broadcast_to(jnp.sum(unit * scaled, axis=1, keepdims=True), (count, HD))

    def gain_copy(i, to):
        return pltpu.make_async_remote_copy(
            src_ref=gp.at[i], dst_ref=gr.at[i], send_sem=gp_sem.at[2 * i],
            recv_sem=gp_sem.at[2 * i + 1], device_id=to, device_id_type=MESH,
        )

    def send_back(n):
        first, count, cols, _ = extent(1, n)
        at = pl.ds(first, count)
        mean = dot_sum[at, :1] * (1.0 / width)
        upstream = g[pl.ds(pl.multiple_of(t * rows + first, count), count), cols]
        dz = upstream.astype(jnp.float32) + inv[at, :1] * (dn[at, cols] - scl[at, cols] * mean)
        dz = jnp.where(s == 0, jnp.zeros_like(dz), dz)
        hop[1, at, cols] = dz.astype(jnp.bfloat16)
        hop_copy(1, n, t).start()

    each(NH, run_norm_back)
    each(NH, send_back)
    spread(1, 0)
    spread(1, 1)
    each(NH, lambda n: run_norm_back(n + NH))
    each(NH, lambda n: send_back(n + NH))
    gain_copy(0, p_core).start()

    def run_tail(n):
        spread(1, n + 2)
        forward(1, n)

    each(2, run_tail)
    gain_copy(0, p_core).wait_recv()
    gp[1] = gp[0] + gr[0]
    gain_copy(1, p_lo).start()
    each(NC - 4, lambda n: run_tail(n + 2))
    forward(1, NC - 2)
    forward(1, NC - 1)
    gain_copy(1, p_lo).wait_recv()
    gp[2] = gp[1] + gr[1]
    gain_out = pltpu.make_async_copy(gp.at[2], out_g, loc_sem.at[0])
    gain_out.start()

    def drain(n):
        collect(0, n)
        collect(1, n)
        st_m(n, t).wait_send()
        st_c(n, t_lo).wait_send()
        st_l(n, t_lo).wait_send()
        st_f(n, t).wait_send()
        for f in range(2):
            rs_core(f, n).wait_send()
            rs_lo(f, n).wait_send()
            hop_copy(f, n, t).wait_send()
            ag(f, n, AG_L, came[f], p_lo).wait_send()
            ag(f, n, AG_C, came[f], p_core).wait_send()
            ag(f, n, AG_F, flip_lo(came[f]), p_core).wait_send()

    each(NC, drain)
    evicted.wait()
    gain_copy(0, p_core).wait_send()
    gain_copy(1, p_lo).wait_send()
    gain_out.wait()


def store(f, b, e, g, to_f, to_b, to_e, to_g, sem):
    copies = [pltpu.make_async_copy(g, to_g, sem.at[3, 0])]
    for i, (src, dst) in enumerate(((f, to_f), (b, to_b), (e, to_e))):
        part = src.shape[1] // 4
        for k in range(4):
            at = pl.ds(k * part, part)
            copies.append(pltpu.make_async_copy(src.at[0, at], dst.at[0, at], sem.at[i, k]))
    for copy in copies:
        copy.start()
    for copy in copies:
        copy.wait()


def shards(sections, arrivals, grads_in, stash, gain, w_query, w_key, w_value, w_out):
    _, tokens, width = arrivals.shape
    nq = w_query.shape[2]
    heads = nq // HD
    rows = tokens // 4
    nw = nq + 2 * HD
    cw = width // NC
    f32, bf16 = jnp.float32, jnp.bfloat16
    scratch = [
        pltpu.VMEM((width, nw), bf16),
        pltpu.VMEM((nq, width), bf16),
        pltpu.VMEM((tokens, width), bf16),
        pltpu.VMEM((tokens, width), bf16),
        pltpu.VMEM((tokens, width), bf16),
        pltpu.VMEM((tokens, width), bf16),
        pltpu.VMEM((tokens, nw), bf16),
        pltpu.VMEM((tokens, nq), bf16),
        pltpu.VMEM((tokens, nq), bf16),
        pltpu.VMEM((tokens, nw), bf16),
        pltpu.VMEM((2 * rows, width), f32),
        pltpu.VMEM((tokens, HD), f32),
        pltpu.VMEM((tokens, HD), f32),
        pltpu.VMEM((1, width), f32),
        pltpu.VMEM((2, tokens, HD), f32),
        pltpu.VMEM((rows, width), f32),
        pltpu.VMEM((rows, HD), f32),
        pltpu.VMEM((rows, width), f32),
        pltpu.VMEM((rows, HD), f32),
        pltpu.VMEM((NC, 2 * rows, cw), bf16),
        pltpu.VMEM((NC, 2 * rows, cw), bf16),
        pltpu.VMEM((NC, rows, cw), bf16),
        pltpu.VMEM((NC, rows, cw), bf16),
        pltpu.VMEM((NC, 2 * rows, cw), bf16),
        pltpu.VMEM((NC, 2 * rows, cw), bf16),
        pltpu.VMEM((NC, rows // 2, 2 * cw), bf16),
        pltpu.VMEM((NC, rows // 2, 2 * cw), bf16),
        pltpu.VMEM((2, rows, width), bf16),
        pltpu.VMEM((3, 1, width), f32),
        pltpu.VMEM((2, 1, width), f32),
        pltpu.SemaphoreType.DMA((7 + nq // 256,)),
        pltpu.SemaphoreType.DMA((KINDS, NC)),
        pltpu.SemaphoreType.DMA((KINDS, NC)),
        pltpu.SemaphoreType.DMA((2,)),
        pltpu.SemaphoreType.DMA((4,)),
    ]
    any_spec = pl.BlockSpec(memory_space=pl.ANY)
    results = (
        jax.ShapeDtypeStruct((1, tokens, width), bf16),
        jax.ShapeDtypeStruct((1, tokens, width), bf16),
        jax.ShapeDtypeStruct((1, rows, width), bf16),
        jax.ShapeDtypeStruct((1, width), f32),
    )
    flops = 2 * tokens * width * (2 * nw + 2 * nq + nw)
    outs = pl.pallas_call(
        functools.partial(kernel, sections, tokens, width, heads),
        out_shape=tuple(pltpu.VMEM(r.shape, r.dtype) for r in results),
        in_specs=[any_spec] * 9,
        out_specs=(any_spec,) * 4,
        scratch_shapes=scratch,
        compiler_params=pltpu.CompilerParams(
            collective_id=0, has_side_effects=True, vmem_limit_bytes=50 * 1024 * 1024
        ),
        cost_estimate=pl.CostEstimate(
            flops=flops, bytes_accessed=2 * width * (2 * nw + 6 * tokens), transcendentals=0
        ),
    )(arrivals, grads_in, stash, gain, w_query, w_key, w_value, w_out, jnp.asarray(rope_tables(tokens)))
    return pl.pallas_call(
        store,
        out_shape=tuple(pltpu.HBM(r.shape, r.dtype) for r in results),
        in_specs=[any_spec] * 4,
        out_specs=(any_spec,) * 4,
        scratch_shapes=[pltpu.SemaphoreType.DMA((4, 4))],
        compiler_params=pltpu.CompilerParams(vmem_limit_bytes=1024 * 1024),
        cost_estimate=pl.CostEstimate(flops=0, bytes_accessed=18 * tokens * width, transcendentals=0),
    )(*outs)


def solution(mesh):
    in_specs = (
        P("section", None, None),
        P("section", None, None),
        P("section", "tp", None),
        P("section", None),
        P("section", None, "tp"),
        P("section", None, "tp"),
        P("section", None, "tp"),
        P("section", "tp", None),
    )
    out_specs = (
        P("section", None, None),
        P("section", None, None),
        P("section", "tp", None),
        P("section", None),
    )
    body = functools.partial(shards, mesh.shape["section"])
    return jax.shard_map(body, mesh=mesh, in_specs=in_specs, out_specs=out_specs, check_vma=False)
```

```python
import functools

import jax
import jax.numpy as jnp
import numpy as np
from jax import lax
from jax.experimental import pallas as pl
from jax.experimental.pallas import tpu as pltpu
from jax.sharding import PartitionSpec as P

HD = 128
LOG2E = 1.4426950408889634
NC = 8
EARLY = 3
PAIR = 4
NH = NC // 2
EPSILON = 1e-05
MESH = pl.DeviceIdType.MESH
NN = (((1,), (0,)), ((), ()))
NT = (((1,), (1,)), ((), ()))
TN = (((0,), (0,)), ((), ()))

ST_M, ST_C, ST_L, ST_F = 0, 1, 2, 3
RS_C, RS_L, HOP, AG_C, AG_L, AG_F = 4, 5, 6, 7, 8, 9
PASS = 6
KINDS = 16


def dot(left, right, dims=NN):
    return lax.dot_general(left, right, dims, preferred_element_type=jnp.float32)


def rope_tables(length):
    half = HD // 2
    frequency = np.exp(np.arange(half, dtype=np.float32) * np.float32(-2.0 * np.log(10000.0) / HD))
    angle = np.arange(length, dtype=np.float32)[:, None] * frequency.astype(np.float32)[None, :]
    cosine, sine = np.cos(angle), np.sin(angle)
    return np.stack(
        [np.concatenate([cosine, cosine], 1), np.concatenate([-sine, sine], 1)]
    ).astype(np.float32)


def kernel(
    sections, tokens, width, heads,
    arr, grd, sth, gain, wq, wk, wv, wo, rope,
    out_f, out_b, evict, out_g,
    w, wob, zf, g, zb, nrm, qkv, ctx, dctx, dqkv, mine, dk, dv, gn, rp, scl, inv, dn, dot_sum,
    sc_f, rc_f, sl_f, rl_f, sc_b, rc_b, sl_b, rl_b, hop, gp, gr,
    loc_sem, send_sem, recv_sem, ev_sem, gp_sem,
):
    nq = heads * HD
    rows = tokens // 4
    cw = width // NC
    s = lax.axis_index("section")
    t = lax.axis_index("tp")
    t_core = t + 1 - 2 * (t % 2)
    t_lo = (t + 2) % 4
    t_diag = (t_core + 2) % 4
    last_z = (s % 4) // 3
    first_z = ((s + 3) % 4) // 3
    t_next = (t + 2 * last_z) % 4
    t_prev = (t + 2 * first_z) % 4
    p_core = (s, t_core)
    p_lo = (s, t_lo)
    p_mir = (sections - 1 - s, t_lo)
    p_next = ((s + 1) % sections, t_next)
    p_prev = ((s + sections - 1) % sections, t_prev)
    p_next_lo = ((s + 1) % sections, (t_next + 2) % 4)
    p_prev_lo = ((s + sections - 1) % sections, (t_prev + 2) % 4)

    def block(index):
        return pl.ds(pl.multiple_of(index * rows, rows), rows)

    def chunk(n):
        return pl.ds(pl.multiple_of(n * cw, cw), cw)

    def remote(src, dst, kind, n, device):
        return pltpu.make_async_remote_copy(
            src_ref=src, dst_ref=dst, send_sem=send_sem.at[kind, n], recv_sem=recv_sem.at[kind, n],
            device_id=device, device_id_type=MESH,
        )

    tile = 256
    tiles = nq // tile

    def load(src, dst, n):
        return pltpu.make_async_copy(src, dst, loc_sem.at[n])

    loads = [
        load(arr.at[0], zf, 0),
        load(gain, gn, 1),
        load(wk.at[0], w.at[:, pl.ds(nq, HD)], 2),
        load(wv.at[0], w.at[:, pl.ds(nq + HD, HD)], 3),
        load(rope, rp, 4),
        load(grd.at[0], g, 5),
        load(wo.at[0], wob, 6),
    ]

    def load_q(n):
        cols = pl.ds(pl.multiple_of(n * tile, tile), tile)
        return load(wq.at[0, :, cols], w.at[:, cols], 7 + n)

    loads[0].start()
    loads[1].start()
    loads[4].start()
    for n in range(tiles):
        load_q(n).start()
    loads[2].start()
    loads[3].start()

    barrier = pltpu.get_barrier_semaphore()
    for device in (p_core, p_lo, p_mir, p_next, p_prev, p_next_lo, p_prev_lo):
        pl.semaphore_signal(barrier, inc=1, device_id=device, device_id_type=MESH)
    pl.semaphore_wait(barrier, 7)

    def st_m(n, at):
        return remote(sth.at[0, :, chunk(n)], zb.at[block(at), chunk(n)], ST_M, n, p_mir)

    def st_c(n, at):
        return remote(zb.at[block(t_lo), chunk(n)], zb.at[block(at), chunk(n)], ST_C, n, p_core)

    def st_l(n, at):
        return remote(zb.at[block(t_lo), chunk(n)], zb.at[block(at), chunk(n)], ST_L, n, p_lo)

    def st_f(n, at):
        return remote(zb.at[block(t), chunk(n)], zb.at[block(at), chunk(n)], ST_F, n, p_core)

    def each(count, body):
        lax.fori_loop(0, count, lambda i, c: (body(i), c)[1], 0)

    each(NC, lambda n: st_m(n, t).start())

    def stash_spread(n):
        st_m(n, t_lo).wait_recv()
        st_l(n, t_lo).start()
        st_c(n, t_lo).start()

    def stash_forward(n):
        st_l(n, t).wait_recv()
        st_f(n, t).start()

    def stash_last(n):
        st_c(n, t_diag).wait_recv()
        st_f(n, t_core).wait_recv()

    evicted = pltpu.make_async_remote_copy(
        src_ref=arr.at[0, block(t_lo)], dst_ref=evict.at[0], send_sem=ev_sem.at[0],
        recv_sem=ev_sem.at[1], device_id=p_mir, device_id_type=MESH,
    )

    evicted.start()

    step = 16

    def normalize(src):
        def body(i):
            at = pl.ds(pl.multiple_of(i * step, step), step)
            x = src[at].astype(jnp.float32)
            inverse = lax.rsqrt(jnp.mean(x * x, axis=-1, keepdims=True) + EPSILON)
            x = src[at].astype(jnp.float32)
            nrm[at] = (x * inverse * gn[...]).astype(jnp.bfloat16)

        each(tokens // step, body)

    def turn(x, sign):
        return x * rp[0] + pltpu.roll(x, HD // 2, 1) * (sign * rp[1])

    def project_q(n):
        cols = pl.ds(pl.multiple_of(n * tile, tile), tile)
        y = dot(nrm[...], w[:, cols])
        y = jnp.concatenate(
            [turn(y[:, i * HD:(i + 1) * HD], 1.0) for i in range(tile // HD)], axis=1
        )
        qkv[:, cols] = y.astype(jnp.bfloat16)

    def project_kv():
        y = dot(nrm[...], w[:, nq:])
        qkv[:, nq:nq + HD] = turn(y[:, :HD], 1.0).astype(jnp.bfloat16)
        qkv[:, nq + HD:] = y[:, HD:].astype(jnp.bfloat16)

    def place(b):
        low = (b % 2 + t % 2) % 2
        high = (b // 2 + t // 2) % 2
        return 2 * low + high

    def put(cols, value):
        for b in range(4):
            ctx[block(place(b)), cols] = value[b * rows:(b + 1) * rows]

    def put_back(cols, value):
        part = rows // 2
        for b in range(4):
            for half in range(2):
                at = place(b)
                at = (at // 2) * 2 * rows + half * rows + (at % 2) * part
                to = pl.ds(pl.multiple_of(at, part), part)
                dqkv[to, cols] = value[b * rows + half * part:b * rows + (half + 1) * part]

    def head_cols(h):
        return pl.ds(pl.multiple_of(h * HD, HD), HD)

    scale = HD ** (-0.5)
    mid = tokens // 2
    bfloat = jnp.bfloat16

    def softmax(scores, axis):
        highest = jnp.max(scores, axis=axis, keepdims=True)
        e = jnp.exp2((scores - highest) * (scale * LOG2E))
        return e * (1.0 / jnp.sum(e, axis=axis, keepdims=True))

    def causal(scores, q_axis):
        q_at = lax.broadcasted_iota(jnp.int32, scores.shape, q_axis)
        k_at = lax.broadcasted_iota(jnp.int32, scores.shape, 1 - q_axis)
        return jnp.where(q_at >= k_at, scores, -jnp.inf)

    def attend(h):
        cols = head_cols(h)
        q, k, v = qkv[:, cols], qkv[:, nq:nq + HD], qkv[:, nq + HD:]
        early = softmax(causal(dot(q[:mid], k[:mid], NT), 0), 1)
        late = dot(q[mid:], k, NT)
        late = softmax(jnp.concatenate([late[:, :mid], causal(late[:, mid:], 0)], axis=1), 1)
        out = jnp.concatenate(
            [dot(early.astype(bfloat), v[:mid]), dot(late.astype(bfloat), v)], axis=0
        )
        put(cols, out.astype(bfloat))

    def attend_back(h):
        cols = head_cols(h)
        q, k, v = qkv[:, cols], qkv[:, nq:nq + HD], qkv[:, nq + HD:]
        dc = dctx[:, cols]

        def half(scores, d_probs):
            probs = softmax(scores, 0)
            inner = jnp.sum(probs * d_probs, axis=0, keepdims=True)
            return probs.astype(bfloat), (probs * (d_probs - inner) * scale).astype(bfloat)

        p_early, s_early = half(causal(dot(k[:mid], q[:mid], NT), 1), dot(v[:mid], dc[:mid], NT))
        late = dot(k, q[mid:], NT)
        late = jnp.concatenate([late[:mid], causal(late[mid:], 1)], axis=0)
        p_late, s_late = half(late, dot(v, dc[mid:], NT))

        def whole(first, second):
            first = jnp.concatenate([first, jnp.zeros_like(first)], axis=0)
            return jnp.concatenate([first, second], axis=1)

        d_scores = whole(s_early, s_late)
        dk[...] += dot(d_scores, q)
        dv[...] += dot(whole(p_early, p_late), dc)
        put_back(cols, turn(dot(d_scores, k, TN), -1.0).astype(bfloat))

    def context_back(n):
        cols = pl.ds(pl.multiple_of(n * tile, tile), tile)
        dctx[:, cols] = dot(g[...], wob[cols, :], NT).astype(jnp.bfloat16)

    sc, rc, sl, rl = (sc_f, sc_b), (rc_f, rc_b), (sl_f, sl_b), (rl_f, rl_b)

    def extent(f, n):
        if f == 0:
            return 0, rows, chunk(n), 0
        half = n // NH
        cols = pl.ds(pl.multiple_of((n % NH) * (width // NH), width // NH), width // NH)
        first = pl.multiple_of(half * (rows // 2), rows // 2)
        return first, rows // 2, cols, pl.multiple_of(half * rows, rows)

    def rs_core(f, n):
        return remote(sc[f].at[n], rc[f].at[n], RS_C + PASS * f, n, p_core)

    def rs_lo(f, n):
        return remote(sl[f].at[n], rl[f].at[n], RS_L + PASS * f, n, p_lo)

    def sum_send(f, n, part):
        sc[f][n] = part[2 * rows:].astype(jnp.bfloat16)
        rs_core(f, n).start()
        mine[:, chunk(n)] = part[:2 * rows]

    def sum_core(n):
        rs_core(0, n).wait_recv()
        total = mine[:, chunk(n)] + rc_f[n].astype(jnp.float32)
        sl_f[n] = total[rows:].astype(jnp.bfloat16)
        rs_lo(0, n).start()
        mine[:rows, chunk(n)] = total[:rows]

    def sum_core_back(n):
        rs_core(1, n).wait_recv()
        total = mine[:, chunk(n)] + rc_b[n].astype(jnp.float32)
        part = rows // 2
        cols = pl.ds(pl.multiple_of((n % 2) * cw, cw), cw)
        for half in range(2):
            at = half * rows
            sl_b[half * NH + n // 2, :, cols] = total[at + part:at + rows].astype(jnp.bfloat16)
            mine[at:at + part, chunk(n)] = total[at:at + part]

    def sum_lo(f, n):
        _, count, cols, at = extent(f, n)
        rs_lo(f, n).wait_recv()
        return mine[pl.ds(at, count), cols] + rl[f][n].astype(jnp.float32)

    outs = (out_f, out_b)
    hops = (p_next, p_prev)
    came = ((t + 2 * first_z) % 4, (t + 2 * last_z) % 4)

    def at_out(f, b, n):
        first, count, cols, _ = extent(f, n)
        return outs[f].at[0, pl.ds(pl.multiple_of(b * rows + first, count), count), cols]

    def hop_copy(f, n, b):
        first, count, cols, _ = extent(f, n)
        src = hop.at[f, pl.ds(first, count), cols]
        return remote(src, at_out(f, b, n), HOP + PASS * f, n, hops[f])

    def far_copy(n, b):
        src = hop.at[0, :, chunk(n)]
        return remote(src, at_out(0, b, n), AG_L, n, p_next_lo)

    def ag(f, n, kind, b, to):
        return remote(at_out(f, b, n), at_out(f, b, n), kind + PASS * f, n, to)

    def flip_core(b):
        return b + 1 - 2 * (b % 2)

    def flip_lo(b):
        return (b + 2) % 4

    def spread(f, n):
        b = came[f]
        hop_copy(f, n, b).wait_recv()
        if f == 1:
            ag(f, n, AG_L, b, p_lo).start()
        ag(f, n, AG_C, b, p_core).start()

    def forward(f, n):
        b = flip_lo(came[f])
        if f == 0:
            far_copy(n, b).wait_recv()
        else:
            ag(f, n, AG_L, b, p_lo).wait_recv()
        ag(f, n, AG_F, b, p_core).start()

    def collect(f, n):
        b = flip_core(came[f])
        ag(f, n, AG_C, b, p_core).wait_recv()
        ag(f, n, AG_F, flip_lo(b), p_core).wait_recv()

    def settle_f(n):
        spread(0, n)
        forward(0, n)

    def finish_f(n):
        y = zf[block(t), chunk(n)].astype(jnp.float32) + sum_lo(0, n)
        y = jnp.where(s == sections - 1, jnp.zeros_like(y), y)
        hop[0, :, chunk(n)] = y.astype(jnp.bfloat16)
        hop_copy(0, n, t).start()
        far_copy(n, t).start()

    def loop(count, body, after):
        def both(i):
            body(i)
            for at, steps in after.items():

                @pl.when(i == at)
                def _():
                    for act, n in steps:
                        act(n)

        each(count, both)

    def heads_of(body):
        def several(i):
            for k in range(PAIR):
                body(PAIR * i + k)

        return several

    loads[0].wait()
    loads[1].wait()
    normalize(zf)
    loads[6].start()
    loads[5].start()
    loads[4].wait()

    def run_project(i):
        load_q(i).wait()
        project_q(i)

    each(tiles, run_project)
    loads[2].wait()
    loads[3].wait()
    project_kv()
    stash_spread(0)
    loop(heads // PAIR, heads_of(attend), {i: [(stash_spread, 2 * i + 1), (stash_spread, 2 * i + 2)] for i in range(2)})
    loads[5].wait()
    loads[6].wait()
    loop(tiles, context_back, {1: [(stash_spread, 5)], 3: [(stash_spread, 6)]})

    def run_out(n):
        sum_send(0, n, dot(ctx[...], wob[:, chunk(n)]))

        @pl.when(n > 0)
        def _():
            sum_core(n - 1)

        @pl.when(n == 2)
        def _():
            stash_spread(NC - 1)

        stash_forward(n)

    each(NC, run_out)
    sum_core(NC - 1)
    each(NC, stash_last)
    normalize(zb)
    finish_f(0)
    finish_f(1)
    loop(tiles, project_q, {i: [(finish_f, i + 2)] for i in range(4)})
    project_kv()
    finish_f(6)
    dk[...] = jnp.zeros_like(dk)
    dv[...] = jnp.zeros_like(dv)
    loop(heads // PAIR, heads_of(attend_back), {0: [(finish_f, 7)]})
    put_back(pl.ds(nq, HD), turn(dk[...], -1.0).astype(jnp.bfloat16))
    put_back(pl.ds(nq + HD, HD), dv[...].astype(jnp.bfloat16))

    def run_d_normed(n):
        sum_send(1, n, dot(dqkv[...], w[chunk(n), :], NT))

        @pl.when(n > 0)
        def _():
            sum_core_back(n - 1)

            @pl.when(n % 2 == 0)
            def _():
                rs_lo(1, n // 2 - 1).start()

    each(NC, run_d_normed)
    sum_core_back(NC - 1)
    for n in range(NH - 1, NC):
        rs_lo(1, n).start()

    def own_scaled(i):
        at = pl.ds(pl.multiple_of(t * rows + i * step, step), step)
        to = pl.ds(pl.multiple_of(i * step, step), step)
        x = zb[at].astype(jnp.float32)
        inverse = lax.rsqrt(jnp.mean(x * x, axis=-1, keepdims=True) + EPSILON)
        x = zb[at].astype(jnp.float32)
        scl[to] = x * inverse
        inv[to] = jnp.broadcast_to(inverse, (step, HD))

    each(rows // step, own_scaled)
    dot_sum[...] = jnp.zeros_like(dot_sum)
    gp[0] = jnp.zeros((1, width), jnp.float32)
    each(EARLY, settle_f)

    def run_norm_back(n):
        first, count, cols, _ = extent(1, n)
        at = pl.ds(first, count)
        d = sum_lo(1, n)
        scaled = scl[at, cols]
        gp[0, :, cols] += jnp.sum(d * scaled, axis=0, keepdims=True)
        unit = d * gn[:, cols]
        dn[at, cols] = unit
        dot_sum[at] += jnp.broadcast_to(jnp.sum(unit * scaled, axis=1, keepdims=True), (count, HD))

    def gain_copy(i, to):
        return pltpu.make_async_remote_copy(
            src_ref=gp.at[i], dst_ref=gr.at[i], send_sem=gp_sem.at[2 * i],
            recv_sem=gp_sem.at[2 * i + 1], device_id=to, device_id_type=MESH,
        )

    def send_back(n):
        first, count, cols, _ = extent(1, n)
        at = pl.ds(first, count)
        mean = dot_sum[at, :1] * (1.0 / width)
        upstream = g[pl.ds(pl.multiple_of(t * rows + first, count), count), cols]
        dz = upstream.astype(jnp.float32) + inv[at, :1] * (dn[at, cols] - scl[at, cols] * mean)
        dz = jnp.where(s == 0, jnp.zeros_like(dz), dz)
        hop[1, at, cols] = dz.astype(jnp.bfloat16)
        hop_copy(1, n, t).start()

    each(NH, run_norm_back)
    each(NH, send_back)
    spread(1, 0)
    spread(1, 1)
    each(NH, lambda n: run_norm_back(n + NH))
    each(NH, lambda n: send_back(n + NH))
    gain_copy(0, p_core).start()

    def run_tail(n):
        spread(1, n + 2)
        forward(1, n)

    each(2, run_tail)
    each(NC - EARLY, lambda n: settle_f(n + EARLY))
    gain_copy(0, p_core).wait_recv()
    gp[1] = gp[0] + gr[0]
    gain_copy(1, p_lo).start()
    each(NC - 4, lambda n: run_tail(n + 2))
    forward(1, NC - 2)
    forward(1, NC - 1)
    gain_copy(1, p_lo).wait_recv()
    gp[2] = gp[1] + gr[1]
    gain_out = pltpu.make_async_copy(gp.at[2], out_g, loc_sem.at[0])
    gain_out.start()

    def drain(n):
        collect(0, n)
        collect(1, n)
        st_m(n, t).wait_send()
        st_c(n, t_lo).wait_send()
        st_l(n, t_lo).wait_send()
        st_f(n, t).wait_send()
        for f in range(2):
            rs_core(f, n).wait_send()
            rs_lo(f, n).wait_send()
            hop_copy(f, n, t).wait_send()
            if f == 0:
                far_copy(n, t).wait_send()
            else:
                ag(f, n, AG_L, came[f], p_lo).wait_send()
            ag(f, n, AG_C, came[f], p_core).wait_send()
            ag(f, n, AG_F, flip_lo(came[f]), p_core).wait_send()

    each(NC, drain)
    evicted.wait()
    gain_copy(0, p_core).wait_send()
    gain_copy(1, p_lo).wait_send()
    gain_out.wait()


def store(f, b, e, g, to_f, to_b, to_e, to_g, sem):
    copies = [pltpu.make_async_copy(g, to_g, sem.at[3, 0])]
    for i, (src, dst) in enumerate(((f, to_f), (b, to_b), (e, to_e))):
        part = src.shape[1] // 4
        for k in range(4):
            at = pl.ds(k * part, part)
            copies.append(pltpu.make_async_copy(src.at[0, at], dst.at[0, at], sem.at[i, k]))
    for copy in copies:
        copy.start()
    for copy in copies:
        copy.wait()


def shards(sections, arrivals, grads_in, stash, gain, w_query, w_key, w_value, w_out):
    _, tokens, width = arrivals.shape
    nq = w_query.shape[2]
    heads = nq // HD
    rows = tokens // 4
    nw = nq + 2 * HD
    cw = width // NC
    f32, bf16 = jnp.float32, jnp.bfloat16
    scratch = [
        pltpu.VMEM((width, nw), bf16),
        pltpu.VMEM((nq, width), bf16),
        pltpu.VMEM((tokens, width), bf16),
        pltpu.VMEM((tokens, width), bf16),
        pltpu.VMEM((tokens, width), bf16),
        pltpu.VMEM((tokens, width), bf16),
        pltpu.VMEM((tokens, nw), bf16),
        pltpu.VMEM((tokens, nq), bf16),
        pltpu.VMEM((tokens, nq), bf16),
        pltpu.VMEM((tokens, nw), bf16),
        pltpu.VMEM((2 * rows, width), f32),
        pltpu.VMEM((tokens, HD), f32),
        pltpu.VMEM((tokens, HD), f32),
        pltpu.VMEM((1, width), f32),
        pltpu.VMEM((2, tokens, HD), f32),
        pltpu.VMEM((rows, width), f32),
        pltpu.VMEM((rows, HD), f32),
        pltpu.VMEM((rows, width), f32),
        pltpu.VMEM((rows, HD), f32),
        pltpu.VMEM((NC, 2 * rows, cw), bf16),
        pltpu.VMEM((NC, 2 * rows, cw), bf16),
        pltpu.VMEM((NC, rows, cw), bf16),
        pltpu.VMEM((NC, rows, cw), bf16),
        pltpu.VMEM((NC, 2 * rows, cw), bf16),
        pltpu.VMEM((NC, 2 * rows, cw), bf16),
        pltpu.VMEM((NC, rows // 2, 2 * cw), bf16),
        pltpu.VMEM((NC, rows // 2, 2 * cw), bf16),
        pltpu.VMEM((2, rows, width), bf16),
        pltpu.VMEM((3, 1, width), f32),
        pltpu.VMEM((2, 1, width), f32),
        pltpu.SemaphoreType.DMA((7 + nq // 256,)),
        pltpu.SemaphoreType.DMA((KINDS, NC)),
        pltpu.SemaphoreType.DMA((KINDS, NC)),
        pltpu.SemaphoreType.DMA((2,)),
        pltpu.SemaphoreType.DMA((4,)),
    ]
    any_spec = pl.BlockSpec(memory_space=pl.ANY)
    results = (
        jax.ShapeDtypeStruct((1, tokens, width), bf16),
        jax.ShapeDtypeStruct((1, tokens, width), bf16),
        jax.ShapeDtypeStruct((1, rows, width), bf16),
        jax.ShapeDtypeStruct((1, width), f32),
    )
    flops = 2 * tokens * width * (2 * nw + 2 * nq + nw)
    outs = pl.pallas_call(
        functools.partial(kernel, sections, tokens, width, heads),
        out_shape=tuple(pltpu.VMEM(r.shape, r.dtype) for r in results),
        in_specs=[any_spec] * 9,
        out_specs=(any_spec,) * 4,
        scratch_shapes=scratch,
        compiler_params=pltpu.CompilerParams(
            collective_id=0, has_side_effects=True, vmem_limit_bytes=50 * 1024 * 1024
        ),
        cost_estimate=pl.CostEstimate(
            flops=flops, bytes_accessed=2 * width * (2 * nw + 6 * tokens), transcendentals=0
        ),
    )(arrivals, grads_in, stash, gain, w_query, w_key, w_value, w_out, jnp.asarray(rope_tables(tokens)))
    return pl.pallas_call(
        store,
        out_shape=tuple(pltpu.HBM(r.shape, r.dtype) for r in results),
        in_specs=[any_spec] * 4,
        out_specs=(any_spec,) * 4,
        scratch_shapes=[pltpu.SemaphoreType.DMA((4, 4))],
        compiler_params=pltpu.CompilerParams(vmem_limit_bytes=1024 * 1024),
        cost_estimate=pl.CostEstimate(flops=0, bytes_accessed=18 * tokens * width, transcendentals=0),
    )(*outs)


def solution(mesh):
    in_specs = (
        P("section", None, None),
        P("section", None, None),
        P("section", "tp", None),
        P("section", None),
        P("section", None, "tp"),
        P("section", None, "tp"),
        P("section", None, "tp"),
        P("section", "tp", None),
    )
    out_specs = (
        P("section", None, None),
        P("section", None, None),
        P("section", "tp", None),
        P("section", None),
    )
    body = functools.partial(shards, mesh.shape["section"])
    return jax.shard_map(body, mesh=mesh, in_specs=in_specs, out_specs=out_specs, check_vma=False)
```

```python
import functools

import jax
import jax.numpy as jnp
import numpy as np
from jax import lax
from jax.experimental import pallas as pl
from jax.experimental.pallas import tpu as pltpu
from jax.sharding import PartitionSpec as P

HD = 128
LOG2E = 1.4426950408889634
NC = 8
EARLY = 3
LAG = 3
PAIR = 4
NH = NC // 2
EPSILON = 1e-05
MESH = pl.DeviceIdType.MESH
NN = (((1,), (0,)), ((), ()))
NT = (((1,), (1,)), ((), ()))
TN = (((0,), (0,)), ((), ()))

ST_M, ST_C, ST_L, ST_F = 0, 1, 2, 3
RS_C, RS_L, HOP, AG_C, AG_L, AG_F = 4, 5, 6, 7, 8, 9
PASS = 6
KINDS = 16


def dot(left, right, dims=NN):
    return lax.dot_general(left, right, dims, preferred_element_type=jnp.float32)


def rope_tables(length):
    half = HD // 2
    frequency = np.exp(np.arange(half, dtype=np.float32) * np.float32(-2.0 * np.log(10000.0) / HD))
    angle = np.arange(length, dtype=np.float32)[:, None] * frequency.astype(np.float32)[None, :]
    cosine, sine = np.cos(angle), np.sin(angle)
    return np.stack(
        [np.concatenate([cosine, cosine], 1), np.concatenate([-sine, sine], 1)]
    ).astype(np.float32)


def kernel(
    sections, tokens, width, heads,
    arr, grd, sth, gain, wq, wk, wv, wo, rope,
    out_f, out_b, evict, out_g,
    w, wob, zf, g, zb, nrm, qkv, ctx, dctx, dqkv, mine, dk, dv, gn, rp, scl, inv, dn, dot_sum,
    sc_f, rc_f, sl_f, rl_f, sc_b, rc_b, sl_b, rl_b, hop, gp, gr,
    loc_sem, send_sem, recv_sem, ev_sem, gp_sem,
):
    nq = heads * HD
    rows = tokens // 4
    cw = width // NC
    s = lax.axis_index("section")
    t = lax.axis_index("tp")
    t_core = t + 1 - 2 * (t % 2)
    t_lo = (t + 2) % 4
    t_diag = (t_core + 2) % 4
    last_z = (s % 4) // 3
    first_z = ((s + 3) % 4) // 3
    t_next = (t + 2 * last_z) % 4
    t_prev = (t + 2 * first_z) % 4
    p_core = (s, t_core)
    p_lo = (s, t_lo)
    p_mir = (sections - 1 - s, t_lo)
    p_next = ((s + 1) % sections, t_next)
    p_prev = ((s + sections - 1) % sections, t_prev)
    p_next_lo = ((s + 1) % sections, (t_next + 2) % 4)
    p_prev_lo = ((s + sections - 1) % sections, (t_prev + 2) % 4)

    def block(index):
        return pl.ds(pl.multiple_of(index * rows, rows), rows)

    def chunk(n):
        return pl.ds(pl.multiple_of(n * cw, cw), cw)

    def remote(src, dst, kind, n, device):
        return pltpu.make_async_remote_copy(
            src_ref=src, dst_ref=dst, send_sem=send_sem.at[kind, n], recv_sem=recv_sem.at[kind, n],
            device_id=device, device_id_type=MESH,
        )

    tile = 256
    tiles = nq // tile

    def load(src, dst, n):
        return pltpu.make_async_copy(src, dst, loc_sem.at[n])

    loads = [
        load(arr.at[0], zf, 0),
        load(gain, gn, 1),
        load(wk.at[0], w.at[:, pl.ds(nq, HD)], 2),
        load(wv.at[0], w.at[:, pl.ds(nq + HD, HD)], 3),
        load(rope, rp, 4),
        load(grd.at[0], g, 5),
        load(wo.at[0], wob, 6),
    ]

    def load_q(n):
        cols = pl.ds(pl.multiple_of(n * tile, tile), tile)
        return load(wq.at[0, :, cols], w.at[:, cols], 7 + n)

    loads[0].start()
    loads[1].start()
    loads[4].start()
    for n in range(tiles):
        load_q(n).start()
    loads[2].start()
    loads[3].start()

    barrier = pltpu.get_barrier_semaphore()
    for device in (p_core, p_lo, p_mir, p_next, p_prev, p_next_lo, p_prev_lo):
        pl.semaphore_signal(barrier, inc=1, device_id=device, device_id_type=MESH)
    pl.semaphore_wait(barrier, 7)

    def st_m(n, at):
        return remote(sth.at[0, :, chunk(n)], zb.at[block(at), chunk(n)], ST_M, n, p_mir)

    def st_c(n, at):
        return remote(zb.at[block(t_lo), chunk(n)], zb.at[block(at), chunk(n)], ST_C, n, p_core)

    def st_l(n, at):
        return remote(zb.at[block(t_lo), chunk(n)], zb.at[block(at), chunk(n)], ST_L, n, p_lo)

    def st_f(n, at):
        return remote(zb.at[block(t), chunk(n)], zb.at[block(at), chunk(n)], ST_F, n, p_core)

    def each(count, body):
        lax.fori_loop(0, count, lambda i, c: (body(i), c)[1], 0)

    each(NC, lambda n: st_m(n, t).start())

    def stash_spread(n):
        st_m(n, t_lo).wait_recv()
        st_l(n, t_lo).start()
        st_c(n, t_lo).start()

    def stash_forward(n):
        st_l(n, t).wait_recv()
        st_f(n, t).start()

    def stash_last(n):
        st_c(n, t_diag).wait_recv()
        st_f(n, t_core).wait_recv()

    evicted = pltpu.make_async_remote_copy(
        src_ref=arr.at[0, block(t_lo)], dst_ref=evict.at[0], send_sem=ev_sem.at[0],
        recv_sem=ev_sem.at[1], device_id=p_mir, device_id_type=MESH,
    )

    evicted.start()

    step = 16

    def normalize(src):
        def body(i):
            at = pl.ds(pl.multiple_of(i * step, step), step)
            x = src[at].astype(jnp.float32)
            inverse = lax.rsqrt(jnp.mean(x * x, axis=-1, keepdims=True) + EPSILON)
            x = src[at].astype(jnp.float32)
            nrm[at] = (x * inverse * gn[...]).astype(jnp.bfloat16)

        each(tokens // step, body)

    def turn(x, sign):
        return x * rp[0] + pltpu.roll(x, HD // 2, 1) * (sign * rp[1])

    def project_q(n):
        cols = pl.ds(pl.multiple_of(n * tile, tile), tile)
        y = dot(nrm[...], w[:, cols])
        y = jnp.concatenate(
            [turn(y[:, i * HD:(i + 1) * HD], 1.0) for i in range(tile // HD)], axis=1
        )
        qkv[:, cols] = y.astype(jnp.bfloat16)

    def project_kv():
        y = dot(nrm[...], w[:, nq:])
        qkv[:, nq:nq + HD] = turn(y[:, :HD], 1.0).astype(jnp.bfloat16)
        qkv[:, nq + HD:] = y[:, HD:].astype(jnp.bfloat16)

    def place(b):
        low = (b % 2 + t % 2) % 2
        high = (b // 2 + t // 2) % 2
        return 2 * low + high

    def put(cols, value):
        for b in range(4):
            ctx[block(place(b)), cols] = value[b * rows:(b + 1) * rows]

    def put_back(cols, value):
        part = rows // 2
        for b in range(4):
            for half in range(2):
                at = place(b)
                at = (at // 2) * 2 * rows + half * rows + (at % 2) * part
                to = pl.ds(pl.multiple_of(at, part), part)
                dqkv[to, cols] = value[b * rows + half * part:b * rows + (half + 1) * part]

    def head_cols(h):
        return pl.ds(pl.multiple_of(h * HD, HD), HD)

    scale = HD ** (-0.5)
    mid = tokens // 2
    bfloat = jnp.bfloat16

    def softmax(scores, axis):
        highest = jnp.max(scores, axis=axis, keepdims=True)
        e = jnp.exp2((scores - highest) * (scale * LOG2E))
        return e * (1.0 / jnp.sum(e, axis=axis, keepdims=True))

    def causal(scores, q_axis):
        q_at = lax.broadcasted_iota(jnp.int32, scores.shape, q_axis)
        k_at = lax.broadcasted_iota(jnp.int32, scores.shape, 1 - q_axis)
        return jnp.where(q_at >= k_at, scores, -jnp.inf)

    def attend(h):
        cols = head_cols(h)
        q, k, v = qkv[:, cols], qkv[:, nq:nq + HD], qkv[:, nq + HD:]
        early = softmax(causal(dot(q[:mid], k[:mid], NT), 0), 1)
        late = dot(q[mid:], k, NT)
        late = softmax(jnp.concatenate([late[:, :mid], causal(late[:, mid:], 0)], axis=1), 1)
        out = jnp.concatenate(
            [dot(early.astype(bfloat), v[:mid]), dot(late.astype(bfloat), v)], axis=0
        )
        put(cols, out.astype(bfloat))

    def attend_back(h):
        cols = head_cols(h)
        q, k, v = qkv[:, cols], qkv[:, nq:nq + HD], qkv[:, nq + HD:]
        dc = dctx[:, cols]

        def half(scores, d_probs):
            probs = softmax(scores, 0)
            inner = jnp.sum(probs * d_probs, axis=0, keepdims=True)
            return probs.astype(bfloat), (probs * (d_probs - inner) * scale).astype(bfloat)

        p_early, s_early = half(causal(dot(k[:mid], q[:mid], NT), 1), dot(v[:mid], dc[:mid], NT))
        late = dot(k, q[mid:], NT)
        late = jnp.concatenate([late[:mid], causal(late[mid:], 1)], axis=0)
        p_late, s_late = half(late, dot(v, dc[mid:], NT))

        def whole(first, second):
            first = jnp.concatenate([first, jnp.zeros_like(first)], axis=0)
            return jnp.concatenate([first, second], axis=1)

        d_scores = whole(s_early, s_late)
        dk[...] += dot(d_scores, q)
        dv[...] += dot(whole(p_early, p_late), dc)
        put_back(cols, turn(dot(d_scores, k, TN), -1.0).astype(bfloat))

    def context_back(n):
        cols = pl.ds(pl.multiple_of(n * tile, tile), tile)
        dctx[:, cols] = dot(g[...], wob[cols, :], NT).astype(jnp.bfloat16)

    sc, rc, sl, rl = (sc_f, sc_b), (rc_f, rc_b), (sl_f, sl_b), (rl_f, rl_b)

    def extent(f, n):
        if f == 0:
            return 0, rows, chunk(n), 0
        half = n // NH
        cols = pl.ds(pl.multiple_of((n % NH) * (width // NH), width // NH), width // NH)
        first = pl.multiple_of(half * (rows // 2), rows // 2)
        return first, rows // 2, cols, pl.multiple_of(half * rows, rows)

    def rs_core(f, n):
        return remote(sc[f].at[n], rc[f].at[n], RS_C + PASS * f, n, p_core)

    def rs_lo(f, n):
        return remote(sl[f].at[n], rl[f].at[n], RS_L + PASS * f, n, p_lo)

    def sum_send(f, n, part):
        sc[f][n] = part[2 * rows:].astype(jnp.bfloat16)
        rs_core(f, n).start()
        mine[:, chunk(n)] = part[:2 * rows]

    def sum_core(n):
        rs_core(0, n).wait_recv()
        total = mine[:, chunk(n)] + rc_f[n].astype(jnp.float32)
        sl_f[n] = total[rows:].astype(jnp.bfloat16)
        rs_lo(0, n).start()
        mine[:rows, chunk(n)] = total[:rows]

    def sum_core_back(n):
        rs_core(1, n).wait_recv()
        total = mine[:, chunk(n)] + rc_b[n].astype(jnp.float32)
        part = rows // 2
        cols = pl.ds(pl.multiple_of((n % 2) * cw, cw), cw)
        for half in range(2):
            at = half * rows
            sl_b[half * NH + n // 2, :, cols] = total[at + part:at + rows].astype(jnp.bfloat16)
            mine[at:at + part, chunk(n)] = total[at:at + part]

    def sum_lo(f, n):
        _, count, cols, at = extent(f, n)
        rs_lo(f, n).wait_recv()
        return mine[pl.ds(at, count), cols] + rl[f][n].astype(jnp.float32)

    outs = (out_f, out_b)
    hops = (p_next, p_prev)
    came = ((t + 2 * first_z) % 4, (t + 2 * last_z) % 4)

    def at_out(f, b, n):
        first, count, cols, _ = extent(f, n)
        return outs[f].at[0, pl.ds(pl.multiple_of(b * rows + first, count), count), cols]

    def hop_copy(f, n, b):
        first, count, cols, _ = extent(f, n)
        src = hop.at[f, pl.ds(first, count), cols]
        return remote(src, at_out(f, b, n), HOP + PASS * f, n, hops[f])

    def far_copy(n, b):
        src = hop.at[0, :, chunk(n)]
        return remote(src, at_out(0, b, n), AG_L, n, p_next_lo)

    def ag(f, n, kind, b, to):
        return remote(at_out(f, b, n), at_out(f, b, n), kind + PASS * f, n, to)

    def flip_core(b):
        return b + 1 - 2 * (b % 2)

    def flip_lo(b):
        return (b + 2) % 4

    def spread(f, n):
        b = came[f]
        hop_copy(f, n, b).wait_recv()
        if f == 1:
            ag(f, n, AG_L, b, p_lo).start()
        ag(f, n, AG_C, b, p_core).start()

    def forward(f, n):
        b = flip_lo(came[f])
        if f == 0:
            far_copy(n, b).wait_recv()
        else:
            ag(f, n, AG_L, b, p_lo).wait_recv()
        ag(f, n, AG_F, b, p_core).start()

    def collect(f, n):
        b = flip_core(came[f])
        ag(f, n, AG_C, b, p_core).wait_recv()
        ag(f, n, AG_F, flip_lo(b), p_core).wait_recv()

    def settle_f(n):
        spread(0, n)
        forward(0, n)

    def finish_f(n):
        y = zf[block(t), chunk(n)].astype(jnp.float32) + sum_lo(0, n)
        y = jnp.where(s == sections - 1, jnp.zeros_like(y), y)
        hop[0, :, chunk(n)] = y.astype(jnp.bfloat16)
        hop_copy(0, n, t).start()
        far_copy(n, t).start()

    def loop(count, body, after):
        def both(i):
            body(i)
            for at, steps in after.items():

                @pl.when(i == at)
                def _():
                    for act, n in steps:
                        act(n)

        each(count, both)

    def heads_of(body):
        def several(i):
            for k in range(PAIR):
                body(PAIR * i + k)

        return several

    loads[0].wait()
    loads[1].wait()
    normalize(zf)
    loads[6].start()
    loads[5].start()
    loads[4].wait()

    def run_project(i):
        load_q(i).wait()
        project_q(i)

    each(tiles, run_project)
    loads[2].wait()
    loads[3].wait()
    project_kv()
    stash_spread(0)
    loop(heads // PAIR, heads_of(attend), {i: [(stash_spread, 2 * i + 1), (stash_spread, 2 * i + 2)] for i in range(2)})
    loads[5].wait()
    loads[6].wait()
    loop(tiles, context_back, {1: [(stash_spread, 5)], 3: [(stash_spread, 6)]})

    def run_out(n):
        sum_send(0, n, dot(ctx[...], wob[:, chunk(n)]))

        @pl.when(n >= LAG)
        def _():
            sum_core(n - LAG)

        @pl.when(n == 2)
        def _():
            stash_spread(NC - 1)

        stash_forward(n)

    each(NC, run_out)
    for n in range(NC - LAG, NC):
        sum_core(n)
    each(NC, stash_last)
    normalize(zb)
    finish_f(0)
    finish_f(1)
    loop(tiles, project_q, {i: [(finish_f, i + 2)] for i in range(4)})
    project_kv()
    finish_f(6)
    dk[...] = jnp.zeros_like(dk)
    dv[...] = jnp.zeros_like(dv)
    loop(heads // PAIR, heads_of(attend_back), {0: [(finish_f, 7)]})
    put_back(pl.ds(nq, HD), turn(dk[...], -1.0).astype(jnp.bfloat16))
    put_back(pl.ds(nq + HD, HD), dv[...].astype(jnp.bfloat16))

    def run_d_normed(n):
        sum_send(1, n, dot(dqkv[...], w[chunk(n), :], NT))

        @pl.when(n >= LAG)
        def _():
            sum_core_back(n - LAG)

            @pl.when((n - LAG) % 2 == 1)
            def _():
                rs_lo(1, (n - LAG) // 2).start()

    each(NC, run_d_normed)
    for n in range(NC - LAG, NC):
        sum_core_back(n)
        if n % 2 == 1 and n < NC - 1:
            rs_lo(1, n // 2).start()
    for n in range(NH - 1, NC):
        rs_lo(1, n).start()

    def own_scaled(i):
        at = pl.ds(pl.multiple_of(t * rows + i * step, step), step)
        to = pl.ds(pl.multiple_of(i * step, step), step)
        x = zb[at].astype(jnp.float32)
        inverse = lax.rsqrt(jnp.mean(x * x, axis=-1, keepdims=True) + EPSILON)
        x = zb[at].astype(jnp.float32)
        scl[to] = x * inverse
        inv[to] = jnp.broadcast_to(inverse, (step, HD))

    each(rows // step, own_scaled)
    dot_sum[...] = jnp.zeros_like(dot_sum)
    gp[0] = jnp.zeros((1, width), jnp.float32)
    each(EARLY, settle_f)

    def run_norm_back(n):
        first, count, cols, _ = extent(1, n)
        at = pl.ds(first, count)
        d = sum_lo(1, n)
        scaled = scl[at, cols]
        gp[0, :, cols] += jnp.sum(d * scaled, axis=0, keepdims=True)
        unit = d * gn[:, cols]
        dn[at, cols] = unit
        dot_sum[at] += jnp.broadcast_to(jnp.sum(unit * scaled, axis=1, keepdims=True), (count, HD))

    def gain_copy(i, to):
        return pltpu.make_async_remote_copy(
            src_ref=gp.at[i], dst_ref=gr.at[i], send_sem=gp_sem.at[2 * i],
            recv_sem=gp_sem.at[2 * i + 1], device_id=to, device_id_type=MESH,
        )

    def send_back(n):
        first, count, cols, _ = extent(1, n)
        at = pl.ds(first, count)
        mean = dot_sum[at, :1] * (1.0 / width)
        upstream = g[pl.ds(pl.multiple_of(t * rows + first, count), count), cols]
        dz = upstream.astype(jnp.float32) + inv[at, :1] * (dn[at, cols] - scl[at, cols] * mean)
        dz = jnp.where(s == 0, jnp.zeros_like(dz), dz)
        hop[1, at, cols] = dz.astype(jnp.bfloat16)
        hop_copy(1, n, t).start()

    each(NH, run_norm_back)
    each(NH, send_back)
    spread(1, 0)
    spread(1, 1)
    each(NH, lambda n: run_norm_back(n + NH))
    each(NH, lambda n: send_back(n + NH))
    gain_copy(0, p_core).start()

    def run_tail(n):
        spread(1, n + 2)
        forward(1, n)

    each(2, run_tail)
    each(NC - EARLY, lambda n: settle_f(n + EARLY))
    gain_copy(0, p_core).wait_recv()
    gp[1] = gp[0] + gr[0]
    gain_copy(1, p_lo).start()
    each(NC - 4, lambda n: run_tail(n + 2))
    forward(1, NC - 2)
    forward(1, NC - 1)
    gain_copy(1, p_lo).wait_recv()
    gp[2] = gp[1] + gr[1]
    gain_out = pltpu.make_async_copy(gp.at[2], out_g, loc_sem.at[0])
    gain_out.start()

    def drain(n):
        collect(0, n)
        collect(1, n)
        st_m(n, t).wait_send()
        st_c(n, t_lo).wait_send()
        st_l(n, t_lo).wait_send()
        st_f(n, t).wait_send()
        for f in range(2):
            rs_core(f, n).wait_send()
            rs_lo(f, n).wait_send()
            hop_copy(f, n, t).wait_send()
            if f == 0:
                far_copy(n, t).wait_send()
            else:
                ag(f, n, AG_L, came[f], p_lo).wait_send()
            ag(f, n, AG_C, came[f], p_core).wait_send()
            ag(f, n, AG_F, flip_lo(came[f]), p_core).wait_send()

    each(NC, drain)
    evicted.wait()
    gain_copy(0, p_core).wait_send()
    gain_copy(1, p_lo).wait_send()
    gain_out.wait()


def store(f, b, e, g, to_f, to_b, to_e, to_g, sem):
    copies = [pltpu.make_async_copy(g, to_g, sem.at[3, 0])]
    for i, (src, dst) in enumerate(((f, to_f), (b, to_b), (e, to_e))):
        part = src.shape[1] // 4
        for k in range(4):
            at = pl.ds(k * part, part)
            copies.append(pltpu.make_async_copy(src.at[0, at], dst.at[0, at], sem.at[i, k]))
    for copy in copies:
        copy.start()
    for copy in copies:
        copy.wait()


def shards(sections, arrivals, grads_in, stash, gain, w_query, w_key, w_value, w_out):
    _, tokens, width = arrivals.shape
    nq = w_query.shape[2]
    heads = nq // HD
    rows = tokens // 4
    nw = nq + 2 * HD
    cw = width // NC
    f32, bf16 = jnp.float32, jnp.bfloat16
    scratch = [
        pltpu.VMEM((width, nw), bf16),
        pltpu.VMEM((nq, width), bf16),
        pltpu.VMEM((tokens, width), bf16),
        pltpu.VMEM((tokens, width), bf16),
        pltpu.VMEM((tokens, width), bf16),
        pltpu.VMEM((tokens, width), bf16),
        pltpu.VMEM((tokens, nw), bf16),
        pltpu.VMEM((tokens, nq), bf16),
        pltpu.VMEM((tokens, nq), bf16),
        pltpu.VMEM((tokens, nw), bf16),
        pltpu.VMEM((2 * rows, width), f32),
        pltpu.VMEM((tokens, HD), f32),
        pltpu.VMEM((tokens, HD), f32),
        pltpu.VMEM((1, width), f32),
        pltpu.VMEM((2, tokens, HD), f32),
        pltpu.VMEM((rows, width), f32),
        pltpu.VMEM((rows, HD), f32),
        pltpu.VMEM((rows, width), f32),
        pltpu.VMEM((rows, HD), f32),
        pltpu.VMEM((NC, 2 * rows, cw), bf16),
        pltpu.VMEM((NC, 2 * rows, cw), bf16),
        pltpu.VMEM((NC, rows, cw), bf16),
        pltpu.VMEM((NC, rows, cw), bf16),
        pltpu.VMEM((NC, 2 * rows, cw), bf16),
        pltpu.VMEM((NC, 2 * rows, cw), bf16),
        pltpu.VMEM((NC, rows // 2, 2 * cw), bf16),
        pltpu.VMEM((NC, rows // 2, 2 * cw), bf16),
        pltpu.VMEM((2, rows, width), bf16),
        pltpu.VMEM((3, 1, width), f32),
        pltpu.VMEM((2, 1, width), f32),
        pltpu.SemaphoreType.DMA((7 + nq // 256,)),
        pltpu.SemaphoreType.DMA((KINDS, NC)),
        pltpu.SemaphoreType.DMA((KINDS, NC)),
        pltpu.SemaphoreType.DMA((2,)),
        pltpu.SemaphoreType.DMA((4,)),
    ]
    any_spec = pl.BlockSpec(memory_space=pl.ANY)
    results = (
        jax.ShapeDtypeStruct((1, tokens, width), bf16),
        jax.ShapeDtypeStruct((1, tokens, width), bf16),
        jax.ShapeDtypeStruct((1, rows, width), bf16),
        jax.ShapeDtypeStruct((1, width), f32),
    )
    flops = 2 * tokens * width * (2 * nw + 2 * nq + nw)
    outs = pl.pallas_call(
        functools.partial(kernel, sections, tokens, width, heads),
        out_shape=tuple(pltpu.VMEM(r.shape, r.dtype) for r in results),
        in_specs=[any_spec] * 9,
        out_specs=(any_spec,) * 4,
        scratch_shapes=scratch,
        compiler_params=pltpu.CompilerParams(
            collective_id=0, has_side_effects=True, vmem_limit_bytes=50 * 1024 * 1024
        ),
        cost_estimate=pl.CostEstimate(
            flops=flops, bytes_accessed=2 * width * (2 * nw + 6 * tokens), transcendentals=0
        ),
    )(arrivals, grads_in, stash, gain, w_query, w_key, w_value, w_out, jnp.asarray(rope_tables(tokens)))
    return pl.pallas_call(
        store,
        out_shape=tuple(pltpu.HBM(r.shape, r.dtype) for r in results),
        in_specs=[any_spec] * 4,
        out_specs=(any_spec,) * 4,
        scratch_shapes=[pltpu.SemaphoreType.DMA((4, 4))],
        compiler_params=pltpu.CompilerParams(vmem_limit_bytes=1024 * 1024),
        cost_estimate=pl.CostEstimate(flops=0, bytes_accessed=18 * tokens * width, transcendentals=0),
    )(*outs)


def solution(mesh):
    in_specs = (
        P("section", None, None),
        P("section", None, None),
        P("section", "tp", None),
        P("section", None),
        P("section", None, "tp"),
        P("section", None, "tp"),
        P("section", None, "tp"),
        P("section", "tp", None),
    )
    out_specs = (
        P("section", None, None),
        P("section", None, None),
        P("section", "tp", None),
        P("section", None),
    )
    body = functools.partial(shards, mesh.shape["section"])
    return jax.shard_map(body, mesh=mesh, in_specs=in_specs, out_specs=out_specs, check_vma=False)
```
